512 devices in a mesh: row: 16 (over y, core), col: 32 (over x, z).
Axes of the slice: x: 4, y: 8, z: 8, core: 2. Of those that a mesh axis runs over, the one named last changes fastest.
Arguments:
- tokens: bfloat16 [4096, 4096], P('row', 'col'), may hold values from -6 to 6
- gate_weight: bfloat16 [4096, 16384], P('row', 'col'), may hold values from -0.1875 to 0.1875
- up_weight: bfloat16 [4096, 16384], P('row', 'col'), may hold values from -0.1875 to 0.1875
- gate_mask: int32 [32, 128], P('row', 'col'), may hold values from 0 to 1, as said below
- up_mask: int32 [32, 128], P('row', 'col'), may hold values from 0 to 1, as said below
- cotangent: bfloat16 [4096, 16384], P('row', 'col'), may hold values from -6 to 6
Outputs:
- hidden: bfloat16 [4096, 16384], P('row', 'col')
- grad_tokens: bfloat16 [4096, 4096], P('row', 'col')
- grad_gate: bfloat16 [4096, 16384], P('row', 'col')
- grad_up: bfloat16 [4096, 16384], P('row', 'col')
The draws below stay inside these ranges and needn't reach their ends.
Inputs may be any that keep to these rules, and one draw needn't show every extreme that they name: `gate_mask`: blocks are aligned 128 x 128 squares; each device's tile of 2 x 4 blocks keeps between 1 and 2 of them, and some tile keeps exactly 2. `up_mask`: as for gate_mask, drawn independently.
All inputs are finite; a program needn't handle non-finite values.
Results may differ from the reference program's by a relative error of at most 0.022.
Values may be sent and summed in bfloat16 or wider, within the bound.
No kernel may reach another device: no remote copies, remote signals or barrier semaphores. Data moves between devices by JAX's collectives and lax.ppermute only.
A program may use at most 128 MiB of HBM per device.

```python
import jax
import jax.numpy as jnp
from jax import lax

D = 4096
FF = 16384
BLK = 128
TOK_ROW = 256
TOKENS = 4096
N_ROW = 16
N_COL = 32


def block_pattern(key):
    row_blocks = D // (N_ROW * BLK)
    col_blocks = FF // (N_COL * BLK)
    per_tile = row_blocks * col_blocks
    tile_count = N_ROW * N_COL
    key_order, key_score = jax.random.split(key)
    order = jax.random.permutation(key_order, tile_count)
    counts = per_tile // 8 + order % (per_tile // 8 + 1)
    scores = jax.random.randint(key_score, (tile_count, per_tile), 0, 1 << 20) * per_tile
    scores = scores + jnp.arange(per_tile, dtype=jnp.int32)[None, :]
    order_rank = jnp.argsort(jnp.argsort(scores, axis=1), axis=1)
    keep = (order_rank < counts[:, None]).astype(jnp.int32)
    keep = keep.reshape(N_ROW, N_COL, row_blocks, col_blocks).transpose(0, 2, 1, 3)
    return keep.reshape(N_ROW * row_blocks, N_COL * col_blocks)


def draw_gate_mask(key, part):
    key = jax.random.fold_in(key, 11)
    return block_pattern(key)


def draw_up_mask(key, part):
    key = jax.random.fold_in(key, 23)
    return block_pattern(key)


def steps_of(own_key, shape, pieces, least, high):
    factor_of, own = 1.0, jax.random.fold_in(own_key, 6)
    for position, blocks in pieces:
        draws = jnp.exp(jax.random.uniform(jax.random.fold_in(own, position), (blocks,), jnp.float32, least / len(pieces), high / len(pieces)))
        factor_of = factor_of * jnp.repeat(draws, shape[position] // blocks).reshape([-1 if axis == position else 1 for axis in range(len(shape))])
    return factor_of


def gaussian(rng, extent, deviation, reach, cuts=(), held_as=jnp.bfloat16):
    result = jax.random.normal(rng, extent, jnp.float32) * deviation
    if len(cuts) > 0:
        result = steps_of(rng, extent, cuts, -0.22, 0.18) * result
    return jnp.clip(result, min=-reach, max=reach).astype(held_as)


def setup_inputs(seed: int = 0) -> dict:
    key_list = jax.random.split(jax.random.key(seed), 7)
    return {
        "tokens": gaussian(key_list[0], (TOKENS, D), 1.0, 6.0, ((0, 16), (1, 32))),
        "gate_weight": gaussian(key_list[1], (D, FF), (D // 4) ** -0.5, 0.1875, ((0, 16), (1, 32))),
        "up_weight": gaussian(key_list[2], (D, FF), (D // 4) ** -0.5, 0.1875, ((0, 16), (1, 32))),
        "gate_mask": draw_gate_mask(jax.random.fold_in(key_list[6], 71), 0),
        "up_mask": draw_up_mask(jax.random.fold_in(key_list[6], 71), 0),
        "cotangent": gaussian(key_list[5], (TOKENS, FF), 1.0, 6.0, ((0, 16), (1, 32))),
    }


def expand_mask(block_mask):
    return jnp.repeat(jnp.repeat(block_mask, BLK, axis=0), BLK, axis=1)


def reference(tokens, gate_weight, up_weight, gate_mask, up_mask, cotangent):
    gate_full = expand_mask(gate_mask)
    up_full = expand_mask(up_mask)
    gate_eff = gate_weight * gate_full.astype(jnp.bfloat16)
    up_eff = up_weight * up_full.astype(jnp.bfloat16)
    gate_value = jnp.dot(tokens, gate_eff, preferred_element_type=jnp.float32)
    up_value = jnp.dot(tokens, up_eff, preferred_element_type=jnp.float32)
    sigma = jax.nn.sigmoid(gate_value)
    hidden = (gate_value * sigma * up_value).astype(jnp.bfloat16)
    cot = cotangent.astype(jnp.float32)
    grad_gval = (cot * up_value * sigma * (1.0 + gate_value * (1.0 - sigma))).astype(jnp.bfloat16)
    grad_uval = (cot * gate_value * sigma).astype(jnp.bfloat16)

    width = FF // N_COL

    def col_step(total, index):
        offset = (index * width).astype(jnp.int32)
        part_g = lax.dynamic_slice_in_dim(grad_gval, offset, width, 1)
        part_u = lax.dynamic_slice_in_dim(grad_uval, offset, width, 1)
        weight_g = lax.dynamic_slice_in_dim(gate_eff, offset, width, 1)
        weight_u = lax.dynamic_slice_in_dim(up_eff, offset, width, 1)
        term = jnp.dot(part_g, weight_g.T, preferred_element_type=jnp.float32)
        term = term + jnp.dot(part_u, weight_u.T, preferred_element_type=jnp.float32)
        rounded = lax.optimization_barrier(term.astype(jnp.bfloat16))
        return total + rounded.astype(jnp.float32), None

    start_tokens = jnp.zeros((TOKENS, D), jnp.float32)
    total_tokens, _ = lax.scan(col_step, start_tokens, jnp.arange(N_COL, dtype=jnp.int32))
    grad_tokens = total_tokens.astype(jnp.bfloat16)

    def row_step(totals, index):
        offset = (index * TOK_ROW).astype(jnp.int32)
        rows_x = lax.dynamic_slice_in_dim(tokens, offset, TOK_ROW, 0)
        rows_g = lax.dynamic_slice_in_dim(grad_gval, offset, TOK_ROW, 0)
        rows_u = lax.dynamic_slice_in_dim(grad_uval, offset, TOK_ROW, 0)
        term_g = lax.optimization_barrier(jnp.dot(rows_x.T, rows_g, preferred_element_type=jnp.float32).astype(jnp.bfloat16))
        term_u = lax.optimization_barrier(jnp.dot(rows_x.T, rows_u, preferred_element_type=jnp.float32).astype(jnp.bfloat16))
        return (totals[0] + term_g.astype(jnp.float32), totals[1] + term_u.astype(jnp.float32)), None

    start_weights = (jnp.zeros((D, FF), jnp.float32), jnp.zeros((D, FF), jnp.float32))
    sums, _ = lax.scan(row_step, start_weights, jnp.arange(N_ROW, dtype=jnp.int32))
    grad_gate = (sums[0] * gate_full.astype(jnp.float32)).astype(jnp.bfloat16)
    grad_up = (sums[1] * up_full.astype(jnp.float32)).astype(jnp.bfloat16)
    return hidden, grad_tokens, grad_gate, grad_up
```

```python
import jax
import jax.numpy as jnp
from jax import lax
from jax.experimental import pallas as pl
from jax.experimental.pallas import tpu as pltpu
from jax.sharding import PartitionSpec as P

BLK = 128
SLOTS = 4
META = SLOTS * BLK
BF = jnp.bfloat16
F32 = jnp.float32
VMEM = pl.BlockSpec(memory_space=pltpu.VMEM)
SMEM = pl.BlockSpec(memory_space=pltpu.SMEM)


def params():
    return pltpu.CompilerParams(vmem_limit_bytes=40 * 1024 * 1024)


def call(kernel, outs, in_specs, scratch=()):
    return pl.pallas_call(
        kernel,
        out_shape=outs,
        in_specs=in_specs,
        out_specs=jax.tree.map(lambda _: VMEM, outs),
        scratch_shapes=list(scratch),
        compiler_params=params(),
    )


def kept(mask_ref):
    cols = mask_ref.shape[1]
    first, second, count = jnp.int32(0), jnp.int32(0), jnp.int32(0)
    for p in range(mask_ref.shape[0] * cols):
        m = mask_ref[p // cols, p % cols]
        on = m == 1
        first = jnp.where(on & (count == 0), p, first)
        second = jnp.where(on & (count == 1), p, second)
        count = count + m
    return first, second, count


def block_of(ref, p, cols):
    r = pl.multiple_of((p // cols) * BLK, BLK)
    c = pl.multiple_of((p % cols) * BLK, BLK)
    return r, c


def pack_kernel(gm_ref, um_ref, gw_ref, uw_ref, out_ref):
    cols = gm_ref.shape[1]
    positions = []
    for t, (m_ref, w_ref) in enumerate(((gm_ref, gw_ref), (um_ref, uw_ref))):
        first, second, count = kept(m_ref)
        for s, (p, on) in enumerate(((first, count >= 1), (second, count >= 2))):
            r, c = block_of(w_ref, p, cols)
            block = w_ref[pl.ds(r, BLK), pl.ds(c, BLK)].astype(F32)
            out_ref[pl.ds((2 * t + s) * BLK, BLK), :] = jnp.where(on, block, 0.0).astype(BF)
            positions.append(p)
    lane = lax.broadcasted_iota(jnp.int32, (out_ref.shape[0] - META, BLK), 1)
    meta = jnp.zeros(lane.shape, jnp.int32)
    for s, p in enumerate(positions):
        meta = jnp.where(lane == s, p, meta)
    out_ref[pl.ds(META, lane.shape[0]), :] = meta.astype(F32).astype(BF)


def front_kernel(cols, idx_ref, x_ref, w_ref, cot_ref, hid_ref, g_ref, wg_ref, acc, gt):
    shards = w_ref.shape[0]
    acc[...] = jnp.zeros_like(acc)
    for n in range(shards):
        for s in range(SLOTS):
            p = idx_ref[n, s]
            a = p % cols + (s // 2) * cols
            acc[a] += jnp.dot(
                x_ref[2 * n + p // cols],
                w_ref[n, pl.ds(s * BLK, BLK), :],
                preferred_element_type=F32,
            )
    for c in range(cols):
        gate, up = acc[c], acc[cols + c]
        lanes = pl.ds(c * BLK, BLK)
        cot = cot_ref[:, lanes].astype(F32)
        sigma = jax.nn.sigmoid(gate)
        hid_ref[:, lanes] = (gate * sigma * up).astype(BF)
        gg = cot * up * sigma * (1.0 + gate * (1.0 - sigma))
        gu = cot * gate * sigma
        g_ref[c] = gg.astype(BF)
        g_ref[cols + c] = gu.astype(BF)
        gt[c] = gg.T.astype(BF)
        gt[cols + c] = gu.T.astype(BF)
    for n in range(shards):
        for s in range(SLOTS):
            p = idx_ref[n, s]
            a = p % cols + (s // 2) * cols
            wg_ref[n, pl.ds(s * BLK, BLK), :] = jnp.dot(
                gt[a], x_ref[2 * n + p // cols], preferred_element_type=F32
            ).astype(BF)


def term_kernel(cols, idx_ref, g_ref, w_ref, out_ref):
    for n in range(w_ref.shape[0]):
        sums = [None, None]
        for s in range(SLOTS):
            p = idx_ref[n, s]
            prod = lax.dot_general(
                g_ref[p % cols + (s // 2) * cols],
                w_ref[n, pl.ds(s * BLK, BLK), :],
                (((1,), (1,)), ((), ())),
                preferred_element_type=F32,
            )
            for r in range(2):
                part = jnp.where(p // cols == r, prod, 0.0)
                sums[r] = part if sums[r] is None else sums[r] + part
        for r in range(2):
            out_ref[2 * n + r] = sums[r].astype(BF)


def sum_kernel(t_ref, out_ref):
    total = t_ref[0].astype(F32)
    for j in range(1, t_ref.shape[0]):
        total = total + t_ref[j].astype(F32)
    out_ref[...] = total.astype(BF)


def unpack_kernel(gm_ref, um_ref, b_ref, gg_ref, gu_ref):
    cols = gm_ref.shape[1]
    for t, (m_ref, o_ref) in enumerate(((gm_ref, gg_ref), (um_ref, gu_ref))):
        o_ref[...] = jnp.zeros_like(o_ref)
        first, second, count = kept(m_ref)
        for s, (p, on) in enumerate(((first, count >= 1), (second, count >= 2))):

            @pl.when(on)
            def _(p=p, s=s):
                r, c = block_of(o_ref, p, cols)
                block = b_ref[pl.ds((2 * t + s) * BLK, BLK), :].astype(F32)
                o_ref[pl.ds(r, BLK), pl.ds(c, BLK)] = block.T.astype(BF)


def body(tokens, gate_weight, up_weight, gate_mask, up_mask, cotangent):
    rows, cols_n = lax.axis_size("row"), lax.axis_size("col")
    tok, width = cotangent.shape
    blocks = gate_mask.shape[1]
    shape = jax.ShapeDtypeStruct

    packed = call(pack_kernel, shape((META + 16, BLK), BF), [SMEM, SMEM, VMEM, VMEM])(
        gate_mask, up_mask, gate_weight, up_weight
    )
    tokens, packed = lax.optimization_barrier((tokens, packed))
    weights = lax.all_gather(packed, "row", axis=0)
    x = lax.all_to_all(jnp.broadcast_to(tokens, (cols_n, *tokens.shape)), "col", 0, 0)
    index = weights[:, META, :SLOTS].astype(jnp.int32)

    hidden, grads, wgrads = call(
        lambda *refs: front_kernel(blocks, *refs),
        (
            shape((tok, width), BF),
            shape((2 * blocks, tok, BLK), BF),
            shape((rows, META, BLK), BF),
        ),
        [SMEM, VMEM, VMEM, VMEM],
        [pltpu.VMEM((2 * blocks, tok, BLK), F32), pltpu.VMEM((2 * blocks, BLK, tok), BF)],
    )(index, x, weights, cotangent)
    summed = lax.psum_scatter(wgrads, "row", scatter_dimension=0)
    terms = call(
        lambda *refs: term_kernel(blocks, *refs),
        shape((cols_n, tok, BLK), BF),
        [SMEM, VMEM, VMEM],
    )(index, grads, weights)
    terms = lax.all_to_all(terms, "col", 0, 0)
    grad_tokens = call(sum_kernel, shape(tokens.shape, BF), [VMEM])(terms)
    grad_gate, grad_up = call(
        unpack_kernel,
        (shape(gate_weight.shape, BF), shape(up_weight.shape, BF)),
        [SMEM, SMEM, VMEM],
    )(gate_mask, up_mask, summed)
    return hidden, grad_tokens, grad_gate, grad_up


def solution(mesh):
    spec = P("row", "col")
    return jax.shard_map(
        body, mesh=mesh, in_specs=(spec,) * 6, out_specs=(spec,) * 4, check_vma=False
    )
```

```python
import jax
import jax.numpy as jnp
from jax import lax
from jax.experimental import pallas as pl
from jax.experimental.pallas import tpu as pltpu
from jax.sharding import Mesh
from jax.sharding import PartitionSpec as P

BLK = 128
SLOTS = 4
META = SLOTS * BLK
ROWS_A = 176
BF = jnp.bfloat16
F32 = jnp.float32
VMEM = pl.BlockSpec(memory_space=pltpu.VMEM)
SMEM = pl.BlockSpec(memory_space=pltpu.SMEM)


def params():
    return pltpu.CompilerParams(vmem_limit_bytes=40 * 1024 * 1024)


def call(kernel, outs, in_specs, scratch=()):
    return pl.pallas_call(
        kernel,
        out_shape=outs,
        in_specs=in_specs,
        out_specs=jax.tree.map(lambda _: VMEM, outs),
        scratch_shapes=list(scratch),
        compiler_params=params(),
    )


def kept(mask_ref):
    cols = mask_ref.shape[1]
    first, second, count = jnp.int32(0), jnp.int32(0), jnp.int32(0)
    for p in range(mask_ref.shape[0] * cols):
        m = mask_ref[p // cols, p % cols]
        on = m == 1
        first = jnp.where(on & (count == 0), p, first)
        second = jnp.where(on & (count == 1), p, second)
        count = count + m
    return first, second, count


def block_of(ref, p, cols):
    r = pl.multiple_of((p // cols) * BLK, BLK)
    c = pl.multiple_of((p % cols) * BLK, BLK)
    return r, c


def pack_kernel(gm_ref, um_ref, tok_ref, gw_ref, uw_ref, out_ref, a_ref, b_ref):
    cols = gm_ref.shape[1]
    positions = []
    for t, (m_ref, w_ref) in enumerate(((gm_ref, gw_ref), (um_ref, uw_ref))):
        first, second, count = kept(m_ref)
        for s, (p, on) in enumerate(((first, count >= 1), (second, count >= 2))):
            r, c = block_of(w_ref, p, cols)
            block = w_ref[pl.ds(r, BLK), pl.ds(c, BLK)].astype(F32)
            out_ref[pl.ds((2 * t + s) * BLK, BLK), :] = jnp.where(on, block, 0.0).astype(BF)
            positions.append(p)
    lane = lax.broadcasted_iota(jnp.int32, (out_ref.shape[0] - META, BLK), 1)
    meta = jnp.zeros(lane.shape, jnp.int32)
    for s, p in enumerate(positions):
        meta = jnp.where(lane == s, p, meta)
    out_ref[pl.ds(META, lane.shape[0]), :] = meta.astype(F32).astype(BF)
    for z in range(a_ref.shape[0]):
        a_ref[z] = tok_ref[pl.ds(0, a_ref.shape[1]), :]
    b_ref[...] = tok_ref[pl.ds(a_ref.shape[1], b_ref.shape[0]), :]


def front_kernel(blocks, me_ref, idx_ref, xa0, xa1, xa2, xa3, xb_ref, w_ref, cot_ref, *rest):
    hid_ref, g_ref, keep_ref, send_ref, x_ref, acc, gt = rest
    my_x, my_c = me_ref[0], me_ref[1]
    shards = w_ref.shape[0]
    zs, xs = xb_ref.shape[:2]
    split = xa0.shape[1]
    for k, xa_ref in enumerate((xa0, xa1, xa2, xa3)):
        first = lax.rem(my_x - k + xs, xs) * zs
        for z in range(zs):
            x_ref[first + z, pl.ds(0, split), :] = xa_ref[z]
            x_ref[first + z, pl.ds(split, xb_ref.shape[2]), :] = xb_ref[z, k]
    acc[...] = jnp.zeros_like(acc)
    for n in range(shards):
        for s in range(SLOTS):
            p = idx_ref[n, s]
            a = p % blocks + (s // 2) * blocks
            acc[a] += jnp.dot(
                x_ref[2 * n + p // blocks],
                w_ref[n, pl.ds(s * BLK, BLK), :],
                preferred_element_type=F32,
            )
    for c in range(blocks):
        gate, up = acc[c], acc[blocks + c]
        lanes = pl.ds(c * BLK, BLK)
        cot = cot_ref[:, lanes].astype(F32)
        sigma = jax.nn.sigmoid(gate)
        hid_ref[:, lanes] = (gate * sigma * up).astype(BF)
        gg = cot * up * sigma * (1.0 + gate * (1.0 - sigma))
        gu = cot * gate * sigma
        g_ref[c] = gg.astype(BF)
        g_ref[blocks + c] = gu.astype(BF)
        gt[c] = gg.T.astype(BF)
        gt[blocks + c] = gu.T.astype(BF)
    for out_ref, core in ((send_ref, 1 - my_c), (keep_ref, my_c)):
        for y in range(shards // 2):
            n = 2 * y + core
            for s in range(SLOTS):
                p = idx_ref[n, s]
                a = p % blocks + (s // 2) * blocks
                out_ref[y, pl.ds(s * BLK, BLK), :] = jnp.dot(
                    gt[a], x_ref[2 * n + p // blocks], preferred_element_type=F32
                ).astype(BF)


def term_kernel(blocks, me_ref, idx_ref, g_ref, w_ref, ta0, ta1, ta2, ta3, tb_ref):
    my_x = me_ref[0]
    zs, xs = tb_ref.shape[:2]
    split = ta0.shape[1]
    for k, ta_ref in enumerate((ta0, ta1, ta2, ta3)):
        first = lax.rem(my_x + k, xs) * (zs // 2)
        for i in range(zs // 2):
            n = first + i
            sums = [None, None]
            for s in range(SLOTS):
                p = idx_ref[n, s]
                prod = lax.dot_general(
                    g_ref[p % blocks + (s // 2) * blocks],
                    w_ref[n, pl.ds(s * BLK, BLK), :],
                    (((1,), (1,)), ((), ())),
                    preferred_element_type=F32,
                )
                for r in range(2):
                    part = jnp.where(p // blocks == r, prod, 0.0)
                    sums[r] = part if sums[r] is None else sums[r] + part
            for r in range(2):
                ta_ref[2 * i + r] = sums[r][:split].astype(BF)
                tb_ref[2 * i + r, k] = sums[r][split:].astype(BF)


def total(parts):
    out = parts[0].astype(F32)
    for part in parts[1:]:
        out = out + part.astype(F32)
    return out


def pair_kernel(a_ref, b_ref, out_ref):
    for y in range(out_ref.shape[0]):
        out_ref[y] = total([a_ref[y], b_ref[y]]).astype(BF)


def middle_kernel(a0, a1, a2, a3, b_ref, oa_ref, ob0, ob1, ob2, ob3):
    for z in range(oa_ref.shape[0]):
        oa_ref[z] = total([a[z] for a in (a0, a1, a2, a3)]).astype(BF)
    for k, ob_ref in enumerate((ob0, ob1, ob2, ob3)):
        ob_ref[...] = total([b_ref[z, k] for z in range(b_ref.shape[0])]).astype(BF)


def last_kernel(a_ref, b0, b1, b2, b3, out_ref):
    split = a_ref.shape[1]
    out_ref[pl.ds(0, split), :] = total([a_ref[z] for z in range(a_ref.shape[0])]).astype(BF)
    out_ref[pl.ds(split, b0.shape[0]), :] = total([b[...] for b in (b0, b1, b2, b3)]).astype(BF)


def unpack_kernel(gm_ref, um_ref, b_ref, gg_ref, gu_ref):
    cols = gm_ref.shape[1]
    for t, (m_ref, o_ref) in enumerate(((gm_ref, gg_ref), (um_ref, gu_ref))):
        o_ref[...] = jnp.zeros_like(o_ref)
        first, second, count = kept(m_ref)
        for s, (p, on) in enumerate(((first, count >= 1), (second, count >= 2))):

            @pl.when(on)
            def _(p=p, s=s):
                r, c = block_of(o_ref, p, cols)
                block = b_ref[pl.ds((2 * t + s) * BLK, BLK), :].astype(F32)
                o_ref[pl.ds(r, BLK), pl.ds(c, BLK)] = block.T.astype(BF)


def shift(x, axis, k):
    size = lax.axis_size(axis)
    return lax.ppermute(x, axis, [(i, (i + k) % size) for i in range(size)])


def round_x(x):
    return [x] + [shift(x, "x", k) for k in (1, 2, 3)]


def body(tokens, gate_weight, up_weight, gate_mask, up_mask, cotangent):
    ys, cs, xs, zs = (lax.axis_size(a) for a in ("y", "c", "x", "z"))
    tok, width = cotangent.shape
    blocks = gate_mask.shape[1]
    split = ROWS_A
    left = tok - split
    shape = jax.ShapeDtypeStruct
    me = jnp.stack([lax.axis_index("x"), lax.axis_index("c")]).astype(jnp.int32)

    packed, half_a, half_b = call(
        pack_kernel,
        (shape((META + 16, BLK), BF), shape((zs, split, BLK), BF), shape((left, BLK), BF)),
        [SMEM, SMEM, VMEM, VMEM, VMEM],
    )(gate_mask, up_mask, tokens, gate_weight, up_weight)
    weights = lax.all_gather(packed, ("y", "c"), axis=0)
    x_b = jnp.stack(round_x(half_b))
    half_a = lax.all_to_all(half_a, "z", 0, 0)
    x_a = round_x(half_a)
    x_b = lax.all_to_all(jnp.broadcast_to(x_b, (zs, *x_b.shape)), "z", 0, 0)
    index = weights[:, META, :SLOTS].astype(jnp.int32)

    hidden, grads, keep, send = call(
        lambda *refs: front_kernel(blocks, *refs),
        (
            shape((tok, width), BF),
            shape((2 * blocks, tok, BLK), BF),
            shape((ys, META, BLK), BF),
            shape((ys, META, BLK), BF),
        ),
        [SMEM, SMEM] + [VMEM] * 7,
        [
            pltpu.VMEM((xs * zs, tok, BLK), BF),
            pltpu.VMEM((2 * blocks, tok, BLK), F32),
            pltpu.VMEM((2 * blocks, BLK, tok), BF),
        ],
    )(me, index, *x_a, x_b, weights, cotangent)
    other = shift(send, "c", 1)
    *t_a, t_b = call(
        lambda *refs: term_kernel(blocks, *refs),
        (shape((zs, split, BLK), BF),) * xs + (shape((zs, xs, left, BLK), BF),),
        [SMEM, SMEM, VMEM, VMEM],
    )(me, index, grads, weights)
    t_a = [t_a[0]] + [shift(t_a[k], "x", k) for k in range(1, xs)]
    wgrads = call(pair_kernel, shape((ys, META, BLK), BF), [VMEM] * 2)(keep, other)
    wgrads = lax.psum_scatter(wgrads, "y", scatter_dimension=0)
    t_b = lax.all_to_all(t_b, "z", 0, 0)
    t_a, *t_b = call(
        middle_kernel,
        (shape((zs, split, BLK), BF),) + (shape((left, BLK), BF),) * xs,
        [VMEM] * 5,
    )(*t_a, t_b)
    t_b = [t_b[0]] + [shift(t_b[k], "x", k) for k in range(1, xs)]
    t_a = lax.all_to_all(t_a, "z", 0, 0)
    grad_tokens = call(last_kernel, shape(tokens.shape, BF), [VMEM] * 5)(t_a, *t_b)
    grad_gate, grad_up = call(
        unpack_kernel,
        (shape(gate_weight.shape, BF), shape(up_weight.shape, BF)),
        [SMEM, SMEM, VMEM],
    )(gate_mask, up_mask, wgrads)
    return hidden, grad_tokens, grad_gate, grad_up


def solution(mesh):
    rows, cols = mesh.devices.shape
    cut = Mesh(mesh.devices.reshape(rows // 2, 2, 4, cols // 4), ("y", "c", "x", "z"))
    spec = P(("y", "c"), ("x", "z"))
    return jax.shard_map(
        body, mesh=cut, in_specs=(spec,) * 6, out_specs=(spec,) * 4, check_vma=False
    )
```

```python
import jax
import jax.numpy as jnp
from jax import lax
from jax.experimental import pallas as pl
from jax.experimental.pallas import tpu as pltpu
from jax.sharding import Mesh
from jax.sharding import PartitionSpec as P

BLK = 128
SLOTS = 4
META = SLOTS * BLK
BF = jnp.bfloat16
F32 = jnp.float32
VMEM = pl.BlockSpec(memory_space=pltpu.VMEM)
SMEM = pl.BlockSpec(memory_space=pltpu.SMEM)
HBM = pl.BlockSpec(memory_space=pltpu.HBM)


def call(kernel, outs, in_specs, scratch=(), out_spec=VMEM, limit=40):
    return pl.pallas_call(
        kernel,
        out_shape=outs,
        in_specs=in_specs,
        out_specs=jax.tree.map(lambda _: out_spec, outs),
        scratch_shapes=list(scratch),
        compiler_params=pltpu.CompilerParams(vmem_limit_bytes=limit * 1024 * 1024),
    )


def kept(mask_ref):
    cols = mask_ref.shape[1]
    first, second, count = jnp.int32(0), jnp.int32(0), jnp.int32(0)
    for p in range(mask_ref.shape[0] * cols):
        m = mask_ref[p // cols, p % cols]
        on = m == 1
        first = jnp.where(on & (count == 0), p, first)
        second = jnp.where(on & (count == 1), p, second)
        count = count + m
    return first, second, count


def block_of(ref, p, cols):
    r = pl.multiple_of((p // cols) * BLK, BLK)
    c = pl.multiple_of((p % cols) * BLK, BLK)
    return r, c


def pack_kernel(gm_ref, um_ref, tok_ref, gw_ref, uw_ref, out_ref, all_ref, gm, um, tail, zero, sems):
    cols = gm.shape[1]
    copies = [
        pltpu.make_async_copy(tok_ref, all_ref.at[z], sems.at[z]) for z in range(all_ref.shape[0])
    ]
    masks = [
        pltpu.make_async_copy(a, b, sems.at[len(copies) + t])
        for t, (a, b) in enumerate(((gm_ref, gm), (um_ref, um)))
    ]
    for copy in masks + copies:
        copy.start()
    zero[...] = jnp.zeros_like(zero)
    for copy in masks:
        copy.wait()
    sem = len(copies) + len(masks)
    positions = []
    for t, (m_ref, w_ref) in enumerate(((gm, gw_ref), (um, uw_ref))):
        first, second, count = kept(m_ref)
        for s, (p, on) in enumerate(((first, count >= 1), (second, count >= 2))):
            r, c = block_of(w_ref, p, cols)
            place = out_ref.at[pl.ds((2 * t + s) * BLK, BLK)]
            block = w_ref.at[pl.ds(r, BLK), pl.ds(c, BLK)]
            copy = pltpu.make_async_copy(block, place, sems.at[sem])
            empty = pltpu.make_async_copy(zero, place, sems.at[sem])
            pl.when(on)(copy.start)
            pl.when(jnp.logical_not(on))(empty.start)
            copies.append(copy)
            positions.append(p)
            sem += 1
    lane = lax.broadcasted_iota(jnp.int32, tail.shape, 1)
    meta = jnp.zeros(lane.shape, jnp.int32)
    for s, p in enumerate(positions):
        meta = jnp.where(lane == s, p, meta)
    tail[...] = meta.astype(F32).astype(BF)
    copy = pltpu.make_async_copy(tail, out_ref.at[pl.ds(META, tail.shape[0])], sems.at[sem])
    copy.start()
    for copy in copies + [copy]:
        copy.wait()


def front_kernel(blocks, me_ref, idx_ref, own, la, lb, ra, rb, oa, ob, w_hbm, cot_ref, *rest):
    hid_ref, g_ref, keep_ref, send_ref, x_ref, acc, gt, w_ref, sem = rest
    fetch = pltpu.make_async_copy(w_hbm, w_ref, sem)
    fetch.start()
    my_x, my_c = me_ref[0], me_ref[1]
    shards = w_ref.shape[0]
    half = la.shape[0]
    xs = x_ref.shape[0] // (2 * half)
    for part, k, z in (
        (own, 0, 0),
        (la, -1, 0),
        (lb, -1, half),
        (ra, 1, 0),
        (rb, 1, half),
        (oa, 2, 0),
        (ob, 2, half),
    ):
        first = lax.rem(my_x + k + xs, xs) * (2 * half) + z
        for i in range(part.shape[0]):
            x_ref[first + i] = part[i]
    fetch.wait()
    acc[...] = jnp.zeros_like(acc)
    for n in range(shards):
        for s in range(SLOTS):
            p = idx_ref[n, s]
            a = p % blocks + (s // 2) * blocks
            acc[a] += jnp.dot(
                x_ref[2 * n + p // blocks],
                w_ref[n, pl.ds(s * BLK, BLK), :],
                preferred_element_type=F32,
            )
    for c in range(blocks):
        gate, up = acc[c], acc[blocks + c]
        lanes = pl.ds(c * BLK, BLK)
        cot = cot_ref[:, lanes].astype(F32)
        sigma = jax.nn.sigmoid(gate)
        hid_ref[:, lanes] = (gate * sigma * up).astype(BF)
        gg = cot * up * sigma * (1.0 + gate * (1.0 - sigma))
        gu = cot * gate * sigma
        g_ref[c] = gg.astype(BF)
        g_ref[blocks + c] = gu.astype(BF)
        gt[c] = gg.T.astype(BF)
        gt[blocks + c] = gu.T.astype(BF)
    for out_ref, core in ((send_ref, 1 - my_c), (keep_ref, my_c)):
        for y in range(shards // 2):
            n = 2 * y + core
            for s in range(SLOTS):
                p = idx_ref[n, s]
                a = p % blocks + (s // 2) * blocks
                out_ref[y, pl.ds(s * BLK, BLK), :] = jnp.dot(
                    gt[a], x_ref[2 * n + p // blocks], preferred_element_type=F32
                ).astype(BF)


def term_kernel(blocks, me_ref, idx_ref, g_ref, w_ref, own, na, nb, pa, pb, oa, ob):
    my_x = me_ref[0]
    half = na.shape[0]
    xs = w_ref.shape[0] // half
    for part, k, z in (
        (oa, 2, 0),
        (ob, 2, half),
        (nb, 1, half),
        (pa, -1, 0),
        (na, 1, 0),
        (pb, -1, half),
        (own, 0, 0),
    ):
        first = lax.rem(my_x + k + xs, xs) * half + z // 2
        for i in range(part.shape[0] // 2):
            n = first + i
            sums = [None, None]
            for s in range(SLOTS):
                p = idx_ref[n, s]
                prod = lax.dot_general(
                    g_ref[p % blocks + (s // 2) * blocks],
                    w_ref[n, pl.ds(s * BLK, BLK), :],
                    (((1,), (1,)), ((), ())),
                    preferred_element_type=F32,
                )
                for r in range(2):
                    add = jnp.where(p // blocks == r, prod, 0.0)
                    sums[r] = add if sums[r] is None else sums[r] + add
            for r in range(2):
                part[2 * i + r] = sums[r].astype(BF)


def total(parts):
    out = parts[0].astype(F32)
    for part in parts[1:]:
        out = out + part.astype(F32)
    return out


def add_kernel(*refs):
    n = len(refs) // 3
    for a, b, out in zip(refs[:n], refs[n : 2 * n], refs[2 * n :], strict=True):
        for i in range(out.shape[0]):
            out[i] = total([a[i], b[i]]).astype(BF)


def middle_kernel(own, la, lb, ra, rb, out_ref):
    half = la.shape[0]
    for i in range(half):
        out_ref[i] = total([own[i], la[i], ra[i]]).astype(BF)
        out_ref[half + i] = total([own[half + i], lb[i], rb[i]]).astype(BF)


def last_kernel(a_ref, out_ref):
    out_ref[...] = total([a_ref[z] for z in range(a_ref.shape[0])]).astype(BF)


def unpack_kernel(gm_ref, um_ref, b_ref, gg_ref, gu_ref):
    cols = gm_ref.shape[1]
    for t, (m_ref, o_ref) in enumerate(((gm_ref, gg_ref), (um_ref, gu_ref))):
        o_ref[...] = jnp.zeros_like(o_ref)
        first, second, count = kept(m_ref)
        for s, (p, on) in enumerate(((first, count >= 1), (second, count >= 2))):

            @pl.when(on)
            def _(p=p, s=s):
                r, c = block_of(o_ref, p, cols)
                block = b_ref[pl.ds((2 * t + s) * BLK, BLK), :].astype(F32)
                o_ref[pl.ds(r, BLK), pl.ds(c, BLK)] = block.T.astype(BF)


def shift(x, axis, k):
    size = lax.axis_size(axis)
    return lax.ppermute(x, axis, [(i, (i + k) % size) for i in range(size)])


def body(tokens, gate_weight, up_weight, gate_mask, up_mask, cotangent):
    ys, cs, xs, zs = (lax.axis_size(a) for a in ("y", "c", "x", "z"))
    tok, width = cotangent.shape
    blocks = gate_mask.shape[1]
    half = zs // 2
    shape = jax.ShapeDtypeStruct
    me = jnp.stack([lax.axis_index("x"), lax.axis_index("c")]).astype(jnp.int32)

    packed, own = call(
        pack_kernel,
        (shape((META + 16, BLK), BF), shape((zs, tok, BLK), BF)),
        [HBM] * 5,
        [
            pltpu.SMEM(gate_mask.shape, jnp.int32),
            pltpu.SMEM(up_mask.shape, jnp.int32),
            pltpu.VMEM((16, BLK), BF),
            pltpu.VMEM((BLK, BLK), BF),
            pltpu.SemaphoreType.DMA((zs + 2 + SLOTS + 1,)),
        ],
        HBM,
        60,
    )(gate_mask, up_mask, tokens, gate_weight, up_weight)
    weights = lax.all_gather(packed, ("y", "c"), axis=0)
    own = lax.all_to_all(own, "z", 0, 0)
    own_a, own_b = own[:half], own[half:]
    la, rb = shift(own_a, "x", 1), shift(own_b, "x", -1)
    lb, ra = shift(own_b, "x", 1), shift(own_a, "x", -1)
    oa, ob = shift(la, "x", 1), shift(rb, "x", -1)
    index = weights[:, META, :SLOTS].astype(jnp.int32)

    hidden, grads, keep, send = call(
        lambda *refs: front_kernel(blocks, *refs),
        (
            shape((tok, width), BF),
            shape((2 * blocks, tok, BLK), BF),
            shape((ys, META, BLK), BF),
            shape((ys, META, BLK), BF),
        ),
        [SMEM, SMEM] + [VMEM] * 7 + [HBM, VMEM],
        [
            pltpu.VMEM((xs * zs, tok, BLK), BF),
            pltpu.VMEM((2 * blocks, tok, BLK), F32),
            pltpu.VMEM((2 * blocks, BLK, tok), BF),
            pltpu.VMEM(weights.shape, BF),
            pltpu.SemaphoreType.DMA(()),
        ],
    )(me, index, own, la, lb, ra, rb, oa, ob, weights, cotangent)
    other = shift(send, "c", 1)
    piece = shape((half, tok, BLK), BF)
    own, na, nb, pa, pb, oa, ob = call(
        lambda *refs: term_kernel(blocks, *refs),
        (shape((zs, tok, BLK), BF),) + (piece,) * 6,
        [SMEM, SMEM, VMEM, VMEM],
    )(me, index, grads, weights)
    oa, ob = shift(oa, "x", 1), shift(ob, "x", -1)
    lb, ra = shift(nb, "x", 1), shift(pa, "x", -1)
    (wgrads,) = call(add_kernel, (shape(keep.shape, BF),), [VMEM] * 2)(keep, other)
    wgrads = lax.psum_scatter(wgrads, "y", scatter_dimension=0)
    na, pb = call(add_kernel, (piece,) * 2, [VMEM] * 4)(na, pb, oa, ob)
    la, rb = shift(na, "x", 1), shift(pb, "x", -1)
    own = call(middle_kernel, shape(own.shape, BF), [VMEM] * 5)(own, la, lb, ra, rb)
    own = lax.all_to_all(own, "z", 0, 0)
    grad_tokens = call(last_kernel, shape(tokens.shape, BF), [VMEM])(own)
    grad_gate, grad_up = call(
        unpack_kernel,
        (shape(gate_weight.shape, BF), shape(up_weight.shape, BF)),
        [SMEM, SMEM, VMEM],
    )(gate_mask, up_mask, wgrads)
    return hidden, grad_tokens, grad_gate, grad_up


def solution(mesh):
    rows, cols = mesh.devices.shape
    cut = Mesh(mesh.devices.reshape(rows // 2, 2, 4, cols // 4), ("y", "c", "x", "z"))
    spec = P(("y", "c"), ("x", "z"))
    return jax.shard_map(
        body, mesh=cut, in_specs=(spec,) * 6, out_specs=(spec,) * 4, check_vma=False
    )
```

```python
import jax
import jax.numpy as jnp
from jax import lax
from jax.experimental import pallas as pl
from jax.experimental.pallas import tpu as pltpu
from jax.sharding import Mesh
from jax.sharding import PartitionSpec as P

BLK = 128
SLOTS = 4
META = SLOTS * BLK
BF = jnp.bfloat16
F32 = jnp.float32
VMEM = pl.BlockSpec(memory_space=pltpu.VMEM)
SMEM = pl.BlockSpec(memory_space=pltpu.SMEM)
HBM = pl.BlockSpec(memory_space=pltpu.HBM)


def call(kernel, outs, in_specs, scratch=(), out_spec=VMEM, limit=40):
    return pl.pallas_call(
        kernel,
        out_shape=outs,
        in_specs=in_specs,
        out_specs=jax.tree.map(lambda _: out_spec, outs),
        scratch_shapes=list(scratch),
        compiler_params=pltpu.CompilerParams(vmem_limit_bytes=limit * 1024 * 1024),
    )


def kept(mask_ref):
    cols = mask_ref.shape[1]
    first, second, count = jnp.int32(0), jnp.int32(0), jnp.int32(0)
    for p in range(mask_ref.shape[0] * cols):
        m = mask_ref[p // cols, p % cols]
        on = m == 1
        first = jnp.where(on & (count == 0), p, first)
        second = jnp.where(on & (count == 1), p, second)
        count = count + m
    return first, second, count


def block_of(ref, p, cols):
    r = pl.multiple_of((p // cols) * BLK, BLK)
    c = pl.multiple_of((p % cols) * BLK, BLK)
    return r, c


def turn(i, stage, size):
    if stage == "far":
        return (i + size // 2) % size
    if stage == "one":
        return i + 1 - 2 * (i % 2)
    return (i + size - 1 + 2 * (i % 2)) % size


def stages(size):
    return (["far"] if size > 4 else []) + ["one", "two"]


def swap(x, axis, stage):
    size = lax.axis_size(axis)
    return lax.ppermute(x, axis, [(i, turn(i, stage, size)) for i in range(size)])


def origin(i, j, size):
    for bit, stage in reversed(list(enumerate(stages(size)))):
        if j >> bit & 1:
            i = turn(i, stage, size)
    return i


def pack_kernel(gm_ref, um_ref, tok_ref, gw_ref, uw_ref, out_ref, all_ref, gm, um, sems):
    cols = gm.shape[1]
    tokens = pltpu.make_async_copy(tok_ref, all_ref.at[0], sems.at[0])
    masks = [
        pltpu.make_async_copy(a, b, sems.at[1 + t])
        for t, (a, b) in enumerate(((gm_ref, gm), (um_ref, um)))
    ]
    for copy in masks + [tokens]:
        copy.start()
    for copy in masks:
        copy.wait()
    chosen = []
    for t, (m_ref, w_ref) in enumerate(((gm, gw_ref), (um, uw_ref))):
        first, second, count = kept(m_ref)
        for s, (p, on) in enumerate(((first, count >= 1), (second, count >= 2))):
            r, c = block_of(w_ref, p, cols)
            place = pl.ds((2 * t + s) * BLK, BLK)
            copy = pltpu.make_async_copy(
                w_ref.at[pl.ds(r, BLK), pl.ds(c, BLK)], out_ref.at[place], sems.at[3 + 2 * t + s]
            )
            copy.start()
            chosen.append((p, on, place, copy))
    lane = lax.broadcasted_iota(jnp.int32, (out_ref.shape[0] - META, BLK), 1)
    meta = jnp.zeros(lane.shape, jnp.int32)
    for s, (p, _, _, _) in enumerate(chosen):
        meta = jnp.where(lane == s, p, meta)
    out_ref[pl.ds(META, lane.shape[0]), :] = meta.astype(F32).astype(BF)
    tokens.wait()
    for z in range(1, all_ref.shape[0]):
        all_ref[z] = all_ref[0]
    for _, on, place, copy in chosen:
        copy.wait()

        @pl.when(jnp.logical_not(on))
        def _(place=place):
            out_ref[place, :] = jnp.zeros((BLK, BLK), BF)


def main_kernel(blocks, me_ref, own, r1, r2, oa, ob, w0, w1, w2, w3, cot_ref, *rest):
    hid_ref, keep_ref, send_ref, t0, t1, t2, ta, tb = rest[:8]
    x_ref, w_ref, at_vec, at_ref, idx_ref, acc, g_ref, gt, sem = rest[8:]
    count = w0.shape[0]
    for g, part in enumerate((w0, w1, w2, w3)):
        for i in range(count):
            meta = part[i, pl.ds(META, 16), :].astype(F32).astype(jnp.int32)
            at_vec[pl.ds(g * count + i, 1), :] = meta[:1]
    scalars = pltpu.make_async_copy(at_vec, at_ref, sem)
    scalars.start()
    my_x, my_c, my_y = me_ref[0], me_ref[1], me_ref[2]
    shards = w_ref.shape[0]
    ys, zs, half = shards // 2, own.shape[0], oa.shape[0]
    xs = 2 * shards // zs
    far, one, two = ((turn(my_x, stage, xs)) for stage in ("far", "one", "two"))
    for part, x, z in ((own, my_x, 0), (r1, one, 0), (r2, two, 0), (oa, far, 0), (ob, far, half)):
        for i in range(part.shape[0]):
            x_ref[x * zs + z + i] = part[i]
    scalars.wait()
    for g, part in enumerate((w0, w1, w2, w3)):
        for i in range(count):
            y = origin(my_y, (g % 2) * count + i, ys)
            n = 2 * y + (my_c if g < 2 else 1 - my_c)
            w_ref[n] = part[i, pl.ds(0, META), :]
            for s in range(SLOTS):
                idx_ref[n, s] = at_ref[g * count + i, s]

    acc[...] = jnp.zeros_like(acc)
    for n in range(shards):
        for s in range(SLOTS):
            p = idx_ref[n, s]
            a = p % blocks + (s // 2) * blocks
            acc[a] += jnp.dot(
                x_ref[2 * n + p // blocks],
                w_ref[n, pl.ds(s * BLK, BLK), :],
                preferred_element_type=F32,
            )
    for c in range(blocks):
        gate, up = acc[c], acc[blocks + c]
        lanes = pl.ds(c * BLK, BLK)
        cot = cot_ref[:, lanes].astype(F32)
        sigma = jax.nn.sigmoid(gate)
        hid_ref[:, lanes] = (gate * sigma * up).astype(BF)
        gg = cot * up * sigma * (1.0 + gate * (1.0 - sigma))
        gu = cot * gate * sigma
        g_ref[c] = gg.astype(BF)
        g_ref[blocks + c] = gu.astype(BF)
        gt[c] = gg.T.astype(BF)
        gt[blocks + c] = gu.T.astype(BF)
    for out_ref, core in ((send_ref, 1 - my_c), (keep_ref, my_c)):
        for j in range(ys):
            n = 2 * origin(my_y, j, ys) + core
            for s in range(SLOTS):
                p = idx_ref[n, s]
                a = p % blocks + (s // 2) * blocks
                out_ref[j, pl.ds(s * BLK, BLK), :] = jnp.dot(
                    gt[a], x_ref[2 * n + p // blocks], preferred_element_type=F32
                ).astype(BF)
    for part, x, z in ((ta, far, 0), (tb, far, half), (t1, one, 0), (t2, two, 0), (t0, my_x, 0)):
        for i in range(part.shape[0] // 2):
            n = x * (zs // 2) + z // 2 + i
            sums = [None, None]
            for s in range(SLOTS):
                p = idx_ref[n, s]
                prod = lax.dot_general(
                    g_ref[p % blocks + (s // 2) * blocks],
                    w_ref[n, pl.ds(s * BLK, BLK), :],
                    (((1,), (1,)), ((), ())),
                    preferred_element_type=F32,
                )
                for r in range(2):
                    add = jnp.where(p // blocks == r, prod, 0.0)
                    sums[r] = add if sums[r] is None else sums[r] + add
            for r in range(2):
                part[2 * i + r] = sums[r].astype(BF)


def total(parts):
    out = parts[0].astype(F32)
    for part in parts[1:]:
        out = out + part.astype(F32)
    return out


def halves_kernel(a_ref, b_ref, lo_ref, hi_ref):
    half = lo_ref.shape[0]
    for i in range(half):
        lo_ref[i] = total([a_ref[i], b_ref[i]]).astype(BF)
        hi_ref[i] = total([a_ref[half + i], b_ref[half + i]]).astype(BF)


def forward_kernel(t1, t2, ra, rb, o1, o2):
    half = ra.shape[0]
    for i in range(half):
        o1[i] = total([t1[i], ra[i]]).astype(BF)
        o1[half + i] = t1[half + i]
        o2[i] = t2[i]
        o2[half + i] = total([t2[half + i], rb[i]]).astype(BF)


def middle_kernel(t0, r1, r2, out_ref):
    for i in range(out_ref.shape[0]):
        out_ref[i] = total([t0[i], r1[i], r2[i]]).astype(BF)


def last_kernel(a_ref, out_ref):
    out_ref[...] = total([a_ref[z] for z in range(a_ref.shape[0])]).astype(BF)


def unpack_kernel(gm_ref, um_ref, a_ref, b_ref, gg_ref, gu_ref):
    cols = gm_ref.shape[1]
    for t, (m_ref, o_ref) in enumerate(((gm_ref, gg_ref), (um_ref, gu_ref))):
        o_ref[...] = jnp.zeros_like(o_ref)
        first, second, count = kept(m_ref)
        for s, (p, on) in enumerate(((first, count >= 1), (second, count >= 2))):

            @pl.when(on)
            def _(p=p, s=s):
                r, c = block_of(o_ref, p, cols)
                rows = pl.ds((2 * t + s) * BLK, BLK)
                block = total([a_ref[0, rows, :], b_ref[0, rows, :]])
                o_ref[pl.ds(r, BLK), pl.ds(c, BLK)] = block.T.astype(BF)


def body(tokens, gate_weight, up_weight, gate_mask, up_mask, cotangent):
    ys, xs, zs = (lax.axis_size(a) for a in ("y", "x", "z"))
    tok, width = cotangent.shape
    blocks = gate_mask.shape[1]
    half = zs // 2
    shape = jax.ShapeDtypeStruct
    me = jnp.stack([lax.axis_index(a) for a in ("x", "c", "y")]).astype(jnp.int32)

    packed, own = call(
        pack_kernel,
        (shape((META + 16, BLK), BF), shape((zs, tok, BLK), BF)),
        [HBM] * 5,
        [
            pltpu.SMEM(gate_mask.shape, jnp.int32),
            pltpu.SMEM(up_mask.shape, jnp.int32),
            pltpu.SemaphoreType.DMA((3 + SLOTS,)),
        ],
        limit=60,
    )(gate_mask, up_mask, tokens, gate_weight, up_weight)
    own = lax.all_to_all(own, "z", 0, 0)
    w = packed[None]
    *early, late = stages(ys)
    for stage in early:
        w = jnp.concatenate([w, swap(w, "y", stage)])
    w_late = swap(w, "y", late)
    r1, r2 = swap(own, "x", "one"), swap(own, "x", "two")
    w = [w, w_late, swap(w, "c", "one"), swap(w_late, "c", "one")]
    oa, ob = swap(r1[:half], "x", "two"), swap(r2[half:], "x", "one")

    whole, piece = shape((zs, tok, BLK), BF), shape((half, tok, BLK), BF)
    hidden, keep, send, t0, t1, t2, ta, tb = call(
        lambda *refs: main_kernel(blocks, *refs),
        (
            shape((tok, width), BF),
            shape((ys, META, BLK), BF),
            shape((ys, META, BLK), BF),
            whole,
            whole,
            whole,
            piece,
            piece,
        ),
        [SMEM] + [VMEM] * 10,
        [
            pltpu.VMEM((xs * zs, tok, BLK), BF),
            pltpu.VMEM((2 * ys, META, BLK), BF),
            pltpu.VMEM((2 * ys, BLK), jnp.int32),
            pltpu.SMEM((2 * ys, BLK), jnp.int32),
            pltpu.SMEM((2 * ys, SLOTS), jnp.int32),
            pltpu.VMEM((2 * blocks, tok, BLK), F32),
            pltpu.VMEM((2 * blocks, tok, BLK), BF),
            pltpu.VMEM((2 * blocks, BLK, tok), BF),
            pltpu.SemaphoreType.DMA(()),
        ],
    )(me, own, r1, r2, oa, ob, *w, cotangent)
    other = swap(send, "c", "one")
    ra, rb = swap(ta, "x", "two"), swap(tb, "x", "one")
    lo = keep
    for stage in reversed(stages(ys)):
        part = shape((lo.shape[0] // 2, *lo.shape[1:]), BF)
        lo, hi = call(halves_kernel, (part, part), [VMEM] * 2)(lo, other)
        other = swap(hi, "y", stage)
    t1, t2 = call(forward_kernel, (whole, whole), [VMEM] * 4)(t1, t2, ra, rb)
    r1, r2 = swap(t1, "x", "one"), swap(t2, "x", "two")
    own = call(middle_kernel, whole, [VMEM] * 3)(t0, r1, r2)
    own = lax.all_to_all(own, "z", 0, 0)
    grad_tokens = call(last_kernel, shape(tokens.shape, BF), [VMEM])(own)
    grad_gate, grad_up = call(
        unpack_kernel,
        (shape(gate_weight.shape, BF), shape(up_weight.shape, BF)),
        [SMEM, SMEM, VMEM, VMEM],
    )(gate_mask, up_mask, lo, other)
    return hidden, grad_tokens, grad_gate, grad_up


def solution(mesh):
    rows, cols = mesh.devices.shape
    cut = Mesh(mesh.devices.reshape(rows // 2, 2, 4, cols // 4), ("y", "c", "x", "z"))
    spec = P(("y", "c"), ("x", "z"))
    return jax.shard_map(
        body, mesh=cut, in_specs=(spec,) * 6, out_specs=(spec,) * 4, check_vma=False
    )
```

```python
import jax
import jax.numpy as jnp
from jax import lax
from jax.experimental import pallas as pl
from jax.experimental.pallas import tpu as pltpu
from jax.sharding import Mesh
from jax.sharding import PartitionSpec as P

BLK = 128
SLOTS = 4
META = SLOTS * BLK
BF = jnp.bfloat16
F32 = jnp.float32
VMEM = pl.BlockSpec(memory_space=pltpu.VMEM)
SMEM = pl.BlockSpec(memory_space=pltpu.SMEM)
HBM = pl.BlockSpec(memory_space=pltpu.HBM)


def call(kernel, outs, in_specs, scratch=(), out_spec=VMEM, limit=24):
    return pl.pallas_call(
        kernel,
        out_shape=outs,
        in_specs=in_specs,
        out_specs=jax.tree.map(lambda _: out_spec, outs),
        scratch_shapes=list(scratch),
        compiler_params=pltpu.CompilerParams(vmem_limit_bytes=limit * 1024 * 1024),
    )


def kept(mask_ref):
    cols = mask_ref.shape[1]
    first, second, count = jnp.int32(0), jnp.int32(0), jnp.int32(0)
    for p in range(mask_ref.shape[0] * cols):
        m = mask_ref[p // cols, p % cols]
        on = m == 1
        first = jnp.where(on & (count == 0), p, first)
        second = jnp.where(on & (count == 1), p, second)
        count = count + m
    return first, second, count


def block_of(ref, p, cols):
    r = pl.multiple_of((p // cols) * BLK, BLK)
    c = pl.multiple_of((p % cols) * BLK, BLK)
    return r, c


def turn(i, stage, size):
    if stage == "far":
        return (i + size // 2) % size
    if stage == "one":
        return i + 1 - 2 * (i % 2)
    return (i + size - 1 + 2 * (i % 2)) % size


def stages(size):
    return (["far"] if size > 4 else []) + ["one", "two"]


def swap(x, axis, stage):
    size = lax.axis_size(axis)
    return lax.ppermute(x, axis, [(i, turn(i, stage, size)) for i in range(size)])


def origin(i, j, size):
    for bit, stage in reversed(list(enumerate(stages(size)))):
        if j >> bit & 1:
            i = turn(i, stage, size)
    return i


def pack_kernel(gm_ref, um_ref, tok_ref, gw_ref, uw_ref, out_ref, all_ref, gm, um, sems):
    cols = gm.shape[1]
    tokens = pltpu.make_async_copy(tok_ref, all_ref.at[0], sems.at[0])
    masks = [
        pltpu.make_async_copy(a, b, sems.at[1 + t])
        for t, (a, b) in enumerate(((gm_ref, gm), (um_ref, um)))
    ]
    for copy in masks + [tokens]:
        copy.start()
    for copy in masks:
        copy.wait()
    chosen = []
    for t, (m_ref, w_ref) in enumerate(((gm, gw_ref), (um, uw_ref))):
        first, second, count = kept(m_ref)
        for s, (p, on) in enumerate(((first, count >= 1), (second, count >= 2))):
            r, c = block_of(w_ref, p, cols)
            place = pl.ds((2 * t + s) * BLK, BLK)
            copy = pltpu.make_async_copy(
                w_ref.at[pl.ds(r, BLK), pl.ds(c, BLK)], out_ref.at[place], sems.at[3 + 2 * t + s]
            )
            copy.start()
            chosen.append((p, on, place, copy))
    lane = lax.broadcasted_iota(jnp.int32, (out_ref.shape[0] - META, BLK), 1)
    meta = jnp.zeros(lane.shape, jnp.int32)
    for s, (p, _, _, _) in enumerate(chosen):
        meta = jnp.where(lane == s, p, meta)
    out_ref[pl.ds(META, lane.shape[0]), :] = meta.astype(F32).astype(BF)
    tokens.wait()
    for z in range(1, all_ref.shape[0]):
        all_ref[z] = all_ref[0]
    for _, on, place, copy in chosen:
        copy.wait()

        @pl.when(jnp.logical_not(on))
        def _(place=place):
            out_ref[place, :] = jnp.zeros((BLK, BLK), BF)


def main_kernel(blocks, me_ref, own, r1, r2, oa, ob, w0, w1, w2, w3, cot_ref, *rest):
    hid_ref, keep_ref, send_ref, t_ref = rest[:4]
    x_ref, w_ref, at_vec, at_ref, idx_ref, acc, g_ref, gt, sem = rest[4:]
    count = w0.shape[0]
    for g, part in enumerate((w0, w1, w2, w3)):
        for i in range(count):
            meta = part[i, pl.ds(META, 16), :].astype(F32).astype(jnp.int32)
            at_vec[pl.ds(g * count + i, 1), :] = meta[:1]
    scalars = pltpu.make_async_copy(at_vec, at_ref, sem)
    scalars.start()
    my_x, my_c, my_y = me_ref[0], me_ref[1], me_ref[2]
    shards = w_ref.shape[0]
    ys, zs, half = shards // 2, own.shape[0], oa.shape[0]
    xs = 2 * shards // zs
    far, one, two = ((turn(my_x, stage, xs)) for stage in ("far", "one", "two"))
    for part, x, z in ((own, my_x, 0), (r1, one, 0), (r2, two, 0), (oa, far, 0), (ob, far, half)):
        for i in range(part.shape[0]):
            x_ref[x * zs + z + i] = part[i]
    scalars.wait()
    for g, part in enumerate((w0, w1, w2, w3)):
        for i in range(count):
            y = origin(my_y, (g % 2) * count + i, ys)
            n = 2 * y + (my_c if g < 2 else 1 - my_c)
            w_ref[n] = part[i, pl.ds(0, META), :]
            for s in range(SLOTS):
                idx_ref[n, s] = at_ref[g * count + i, s]

    acc[...] = jnp.zeros_like(acc)
    for n in range(shards):
        for s in range(SLOTS):
            p = idx_ref[n, s]
            a = p % blocks + (s // 2) * blocks
            acc[a] += jnp.dot(
                x_ref[2 * n + p // blocks],
                w_ref[n, pl.ds(s * BLK, BLK), :],
                preferred_element_type=F32,
            )
    for c in range(blocks):
        gate, up = acc[c], acc[blocks + c]
        lanes = pl.ds(c * BLK, BLK)
        cot = cot_ref[:, lanes].astype(F32)
        sigma = jax.nn.sigmoid(gate)
        hid_ref[:, lanes] = (gate * sigma * up).astype(BF)
        gg = cot * up * sigma * (1.0 + gate * (1.0 - sigma))
        gu = cot * gate * sigma
        g_ref[c] = gg.astype(BF)
        g_ref[blocks + c] = gu.astype(BF)
        gt[c] = gg.T.astype(BF)
        gt[blocks + c] = gu.T.astype(BF)
    for out_ref, core in ((send_ref, 1 - my_c), (keep_ref, my_c)):
        for j in range(ys):
            n = 2 * origin(my_y, j, ys) + core
            for s in range(SLOTS):
                p = idx_ref[n, s]
                a = p % blocks + (s // 2) * blocks
                out_ref[j, pl.ds(s * BLK, BLK), :] = jnp.dot(
                    gt[a], x_ref[2 * n + p // blocks], preferred_element_type=F32
                ).astype(BF)
    for n in range(shards):
        sums = [None, None]
        for s in range(SLOTS):
            p = idx_ref[n, s]
            prod = lax.dot_general(
                g_ref[p % blocks + (s // 2) * blocks],
                w_ref[n, pl.ds(s * BLK, BLK), :],
                (((1,), (1,)), ((), ())),
                preferred_element_type=F32,
            )
            for r in range(2):
                add = jnp.where(p // blocks == r, prod, 0.0)
                sums[r] = add if sums[r] is None else sums[r] + add
        for r in range(2):
            k = 2 * n + r
            t_ref[k // zs, k % zs] = sums[r].astype(BF)


def total(parts):
    out = parts[0].astype(F32)
    for part in parts[1:]:
        out = out + part.astype(F32)
    return out


def halves_kernel(a_ref, b_ref, lo_ref, hi_ref):
    half = lo_ref.shape[0]
    for i in range(half):
        lo_ref[i] = total([a_ref[i], b_ref[i]]).astype(BF)
        hi_ref[i] = total([a_ref[half + i], b_ref[half + i]]).astype(BF)


def middle_kernel(t_ref, _, out_ref):
    for z in range(out_ref.shape[0]):
        out_ref[z] = total([t_ref[x, z] for x in range(t_ref.shape[0])]).astype(BF)


def last_kernel(a_ref, out_ref):
    out_ref[...] = total([a_ref[z] for z in range(a_ref.shape[0])]).astype(BF)


def unpack_kernel(gm_ref, um_ref, a_ref, b_ref, gg_ref, gu_ref):
    cols = gm_ref.shape[1]
    for t, (m_ref, o_ref) in enumerate(((gm_ref, gg_ref), (um_ref, gu_ref))):
        o_ref[...] = jnp.zeros_like(o_ref)
        first, second, count = kept(m_ref)
        for s, (p, on) in enumerate(((first, count >= 1), (second, count >= 2))):

            @pl.when(on)
            def _(p=p, s=s):
                r, c = block_of(o_ref, p, cols)
                rows = pl.ds((2 * t + s) * BLK, BLK)
                block = total([a_ref[0, rows, :], b_ref[0, rows, :]])
                o_ref[pl.ds(r, BLK), pl.ds(c, BLK)] = block.T.astype(BF)


def body(tokens, gate_weight, up_weight, gate_mask, up_mask, cotangent):
    ys, xs, zs = (lax.axis_size(a) for a in ("y", "x", "z"))
    tok, width = cotangent.shape
    blocks = gate_mask.shape[1]
    half = zs // 2
    shape = jax.ShapeDtypeStruct
    me = jnp.stack([lax.axis_index(a) for a in ("x", "c", "y")]).astype(jnp.int32)

    packed, own = call(
        pack_kernel,
        (shape((META + 16, BLK), BF), shape((zs, tok, BLK), BF)),
        [HBM] * 5,
        [
            pltpu.SMEM(gate_mask.shape, jnp.int32),
            pltpu.SMEM(up_mask.shape, jnp.int32),
            pltpu.SemaphoreType.DMA((3 + SLOTS,)),
        ],
        limit=60,
    )(gate_mask, up_mask, tokens, gate_weight, up_weight)
    own = lax.all_to_all(own, "z", 0, 0)
    w = packed[None]
    *early, late = stages(ys)
    for stage in early:
        w = jnp.concatenate([w, swap(w, "y", stage)])
    w_late = swap(w, "y", late)
    r1, r2 = swap(own, "x", "one"), swap(own, "x", "two")
    w = [w, w_late, swap(w, "c", "one"), swap(w_late, "c", "one")]
    oa, ob = swap(r1[:half], "x", "two"), swap(r2[half:], "x", "one")

    hidden, keep, send, terms = call(
        lambda *refs: main_kernel(blocks, *refs),
        (
            shape((tok, width), BF),
            shape((ys, META, BLK), BF),
            shape((ys, META, BLK), BF),
            shape((xs, zs, tok, BLK), BF),
        ),
        [SMEM] + [VMEM] * 10,
        [
            pltpu.VMEM((xs * zs, tok, BLK), BF),
            pltpu.VMEM((2 * ys, META, BLK), BF),
            pltpu.VMEM((2 * ys, BLK), jnp.int32),
            pltpu.SMEM((2 * ys, BLK), jnp.int32),
            pltpu.SMEM((2 * ys, SLOTS), jnp.int32),
            pltpu.VMEM((2 * blocks, tok, BLK), F32),
            pltpu.VMEM((2 * blocks, tok, BLK), BF),
            pltpu.VMEM((2 * blocks, BLK, tok), BF),
            pltpu.SemaphoreType.DMA(()),
        ],
    )(me, own, r1, r2, oa, ob, *w, cotangent)
    other = swap(send, "c", "one")
    terms = lax.all_to_all(terms, "x", 0, 0)
    lo = keep
    for stage in reversed(stages(ys)):
        part = shape((lo.shape[0] // 2, *lo.shape[1:]), BF)
        lo, hi = call(halves_kernel, (part, part), [VMEM] * 2)(lo, other)
        other = swap(hi, "y", stage)
    own = call(middle_kernel, shape(own.shape, BF), [VMEM, HBM])(terms, lo)
    own = lax.all_to_all(own, "z", 0, 0)
    grad_tokens = call(last_kernel, shape(tokens.shape, BF), [VMEM])(own)
    grad_gate, grad_up = call(
        unpack_kernel,
        (shape(gate_weight.shape, BF), shape(up_weight.shape, BF)),
        [SMEM, SMEM, VMEM, VMEM],
    )(gate_mask, up_mask, lo, other)
    return hidden, grad_tokens, grad_gate, grad_up


def solution(mesh):
    rows, cols = mesh.devices.shape
    cut = Mesh(mesh.devices.reshape(rows // 2, 2, 4, cols // 4), ("y", "c", "x", "z"))
    spec = P(("y", "c"), ("x", "z"))
    return jax.shard_map(
        body, mesh=cut, in_specs=(spec,) * 6, out_specs=(spec,) * 4, check_vma=False
    )
```

```python
import jax
import jax.numpy as jnp
from jax import lax
from jax.experimental import pallas as pl
from jax.experimental.pallas import tpu as pltpu
from jax.sharding import Mesh
from jax.sharding import PartitionSpec as P

BLK = 128
SLOTS = 4
META = SLOTS * BLK
BF = jnp.bfloat16
F32 = jnp.float32
VMEM = pl.BlockSpec(memory_space=pltpu.VMEM)
SMEM = pl.BlockSpec(memory_space=pltpu.SMEM)
HBM = pl.BlockSpec(memory_space=pltpu.HBM)


def call(kernel, outs, in_specs, scratch=(), out_spec=VMEM, limit=17):
    return pl.pallas_call(
        kernel,
        out_shape=outs,
        in_specs=in_specs,
        out_specs=jax.tree.map(lambda _: out_spec, outs),
        scratch_shapes=list(scratch),
        compiler_params=pltpu.CompilerParams(vmem_limit_bytes=limit * 1024 * 1024),
    )


def kept(mask_ref):
    cols = mask_ref.shape[1]
    first, second, count = jnp.int32(0), jnp.int32(0), jnp.int32(0)
    for p in range(mask_ref.shape[0] * cols):
        m = mask_ref[p // cols, p % cols]
        on = m == 1
        first = jnp.where(on & (count == 0), p, first)
        second = jnp.where(on & (count == 1), p, second)
        count = count + m
    return first, second, count


def block_of(ref, p, cols):
    r = pl.multiple_of((p // cols) * BLK, BLK)
    c = pl.multiple_of((p % cols) * BLK, BLK)
    return r, c


def turn(i, stage, size):
    if stage == "far":
        return (i + size // 2) % size
    if stage == "one":
        return i + 1 - 2 * (i % 2)
    return (i + size - 1 + 2 * (i % 2)) % size


def stages(size):
    return (["far"] if size > 4 else []) + ["one", "two"]


ORDERS = (["far", "one", "two"], ["far", "two", "one"])


def swap(x, axis, stage):
    size = lax.axis_size(axis)
    return lax.ppermute(x, axis, [(i, turn(i, stage, size)) for i in range(size)])


def origin(i, j, size, order=None):
    for bit, stage in reversed(list(enumerate(order or stages(size)))):
        if j >> bit & 1:
            i = turn(i, stage, size)
    return i


def pack_kernel(gm_ref, um_ref, tok_ref, gw_ref, uw_ref, out_ref, all_ref, gm, um, sems):
    cols = gm.shape[1]
    tokens = pltpu.make_async_copy(tok_ref, all_ref.at[0], sems.at[0])
    masks = [
        pltpu.make_async_copy(a, b, sems.at[1 + t])
        for t, (a, b) in enumerate(((gm_ref, gm), (um_ref, um)))
    ]
    for copy in masks + [tokens]:
        copy.start()
    for copy in masks:
        copy.wait()
    chosen = []
    for t, (m_ref, w_ref) in enumerate(((gm, gw_ref), (um, uw_ref))):
        first, second, count = kept(m_ref)
        for s, (p, on) in enumerate(((first, count >= 1), (second, count >= 2))):
            r, c = block_of(w_ref, p, cols)
            place = pl.ds((2 * t + s) * BLK, BLK)
            copy = pltpu.make_async_copy(
                w_ref.at[pl.ds(r, BLK), pl.ds(c, BLK)], out_ref.at[place], sems.at[3 + 2 * t + s]
            )
            copy.start()
            chosen.append((p, on, place, copy))
    lane = lax.broadcasted_iota(jnp.int32, (out_ref.shape[0] - META, BLK), 1)
    meta = jnp.zeros(lane.shape, jnp.int32)
    for s, (p, _, _, _) in enumerate(chosen):
        meta = jnp.where(lane == s, p, meta)
    out_ref[pl.ds(META, lane.shape[0]), :] = meta.astype(F32).astype(BF)
    tokens.wait()
    for z in range(1, all_ref.shape[0]):
        all_ref[z] = all_ref[0]
    for _, on, place, copy in chosen:
        copy.wait()

        @pl.when(jnp.logical_not(on))
        def _(place=place):
            out_ref[place, :] = jnp.zeros((BLK, BLK), BF)


def main_kernel(blocks, me_ref, own, r1, r2, oa, ob, w0, w1, w2, w3, cot_ref, *rest):
    hid_ref, keep_ref, send_ref, t_ref = rest[:4]
    x_ref, w_ref, at_vec, at_ref, idx_ref, acc, g_ref, gt, sem = rest[4:]
    count = w0.shape[0]
    for g, part in enumerate((w0, w1, w2, w3)):
        for i in range(count):
            meta = part[i, pl.ds(META, 16), :].astype(F32).astype(jnp.int32)
            at_vec[pl.ds(g * count + i, 1), :] = meta[:1]
    scalars = pltpu.make_async_copy(at_vec, at_ref, sem)
    scalars.start()
    my_x, my_c, my_y = me_ref[0], me_ref[1], me_ref[2]
    shards = w_ref.shape[0]
    ys, zs, half = shards // 2, own.shape[0], oa.shape[0]
    xs = 2 * shards // zs
    far, one, two = ((turn(my_x, stage, xs)) for stage in ("far", "one", "two"))
    for part, x, z in ((own, my_x, 0), (r1, one, 0), (r2, two, 0), (oa, far, 0), (ob, far, half)):
        for i in range(part.shape[0]):
            x_ref[x * zs + z + i] = part[i]
    scalars.wait()
    for g, part in enumerate((w0, w1, w2, w3)):
        for i in range(count):
            y = origin(my_y, (g % 2) * count + i, ys)
            n = 2 * y + (my_c if g < 2 else 1 - my_c)
            w_ref[n] = part[i, pl.ds(0, META), :]
            for s in range(SLOTS):
                idx_ref[n, s] = at_ref[g * count + i, s]

    acc[...] = jnp.zeros_like(acc)
    for n in range(shards):
        for s in range(SLOTS):
            p = idx_ref[n, s]
            a = p % blocks + (s // 2) * blocks
            acc[a] += jnp.dot(
                x_ref[2 * n + p // blocks],
                w_ref[n, pl.ds(s * BLK, BLK), :],
                preferred_element_type=F32,
            )
    for c in range(blocks):
        gate, up = acc[c], acc[blocks + c]
        lanes = pl.ds(c * BLK, BLK)
        cot = cot_ref[:, lanes].astype(F32)
        sigma = jax.nn.sigmoid(gate)
        hid_ref[:, lanes] = (gate * sigma * up).astype(BF)
        gg = cot * up * sigma * (1.0 + gate * (1.0 - sigma))
        gu = cot * gate * sigma
        g_ref[c] = gg.astype(BF)
        g_ref[blocks + c] = gu.astype(BF)
        gt[c] = gg.T.astype(BF)
        gt[blocks + c] = gu.T.astype(BF)
    for out_ref, core in ((send_ref, 1 - my_c), (keep_ref, my_c)):
        for t, order in enumerate(ORDERS):
            for j, s in ((j, s) for j in range(ys) for s in (2 * t, 2 * t + 1)):
                n = 2 * origin(my_y, j, ys, order) + core
                p = idx_ref[n, s]
                a = p % blocks + t * blocks
                out_ref[t, j, pl.ds((s - 2 * t) * BLK, BLK), :] = jnp.dot(
                    gt[a], x_ref[2 * n + p // blocks], preferred_element_type=F32
                ).astype(BF)
    for n in range(shards):
        sums = [None, None]
        for s in range(SLOTS):
            p = idx_ref[n, s]
            prod = lax.dot_general(
                g_ref[p % blocks + (s // 2) * blocks],
                w_ref[n, pl.ds(s * BLK, BLK), :],
                (((1,), (1,)), ((), ())),
                preferred_element_type=F32,
            )
            for r in range(2):
                add = jnp.where(p // blocks == r, prod, 0.0)
                sums[r] = add if sums[r] is None else sums[r] + add
        for r in range(2):
            k = 2 * n + r
            t_ref[k // zs, k % zs] = sums[r].astype(BF)


def total(parts):
    out = parts[0].astype(F32)
    for part in parts[1:]:
        out = out + part.astype(F32)
    return out


def halves(a_ref, b_ref, lo_ref, hi_ref):
    half = lo_ref.shape[0]
    for i in range(half):
        lo_ref[i] = total([a_ref[i], b_ref[i]]).astype(BF)
        hi_ref[i] = total([a_ref[half + i], b_ref[half + i]]).astype(BF)


def first_kernel(keep, other, lo_g, hi_g, lo_u, hi_u):
    halves(keep.at[0], other.at[0], lo_g, hi_g)
    halves(keep.at[1], other.at[1], lo_u, hi_u)


def second_kernel(g, from_g, u, from_u, lo_g, hi_g, lo_u, hi_u):
    halves(g, from_g, lo_g, hi_g)
    halves(u, from_u, lo_u, hi_u)


def third_kernel(g, from_g, u, from_u, lo, hi):
    halves(g, from_g, lo.at[pl.ds(0, 1)], hi.at[pl.ds(0, 1)])
    halves(u, from_u, lo.at[pl.ds(1, 1)], hi.at[pl.ds(1, 1)])


def middle_kernel(t_ref, _, out_ref):
    for z in range(out_ref.shape[0]):
        out_ref[z] = total([t_ref[x, z] for x in range(t_ref.shape[0])]).astype(BF)


def last_kernel(a_ref, out_ref):
    out_ref[...] = total([a_ref[z] for z in range(a_ref.shape[0])]).astype(BF)


def unpack_kernel(gm_ref, um_ref, a_ref, b_ref, gg_ref, gu_ref):
    cols = gm_ref.shape[1]
    for t, (m_ref, o_ref) in enumerate(((gm_ref, gg_ref), (um_ref, gu_ref))):
        o_ref[...] = jnp.zeros_like(o_ref)
        first, second, count = kept(m_ref)
        for s, (p, on) in enumerate(((first, count >= 1), (second, count >= 2))):

            @pl.when(on)
            def _(p=p, s=s):
                r, c = block_of(o_ref, p, cols)
                rows = pl.ds(s * BLK, BLK)
                block = total([a_ref[t, rows, :], b_ref[t, rows, :]])
                o_ref[pl.ds(r, BLK), pl.ds(c, BLK)] = block.T.astype(BF)


def body(tokens, gate_weight, up_weight, gate_mask, up_mask, cotangent):
    ys, xs, zs = (lax.axis_size(a) for a in ("y", "x", "z"))
    tok, width = cotangent.shape
    blocks = gate_mask.shape[1]
    half = zs // 2
    shape = jax.ShapeDtypeStruct
    me = jnp.stack([lax.axis_index(a) for a in ("x", "c", "y")]).astype(jnp.int32)

    packed, own = call(
        pack_kernel,
        (shape((META + 16, BLK), BF), shape((zs, tok, BLK), BF)),
        [HBM] * 5,
        [
            pltpu.SMEM(gate_mask.shape, jnp.int32),
            pltpu.SMEM(up_mask.shape, jnp.int32),
            pltpu.SemaphoreType.DMA((3 + SLOTS,)),
        ],
        limit=60,
    )(gate_mask, up_mask, tokens, gate_weight, up_weight)
    own = lax.all_to_all(own, "z", 0, 0)
    w = packed[None]
    *early, late = stages(ys)
    for stage in early:
        w = jnp.concatenate([w, swap(w, "y", stage)])
    w_late = swap(w, "y", late)
    r1, r2 = swap(own, "x", "one"), swap(own, "x", "two")
    w = [w, w_late, swap(w, "c", "one"), swap(w_late, "c", "one")]
    oa, ob = swap(r1[:half], "x", "two"), swap(r2[half:], "x", "one")

    hidden, keep, send, terms = call(
        lambda *refs: main_kernel(blocks, *refs),
        (
            shape((tok, width), BF),
            shape((2, ys, META // 2, BLK), BF),
            shape((2, ys, META // 2, BLK), BF),
            shape((xs, zs, tok, BLK), BF),
        ),
        [SMEM] + [VMEM] * 10,
        [
            pltpu.VMEM((xs * zs, tok, BLK), BF),
            pltpu.VMEM((2 * ys, META, BLK), BF),
            pltpu.VMEM((2 * ys, BLK), jnp.int32),
            pltpu.SMEM((2 * ys, BLK), jnp.int32),
            pltpu.SMEM((2 * ys, SLOTS), jnp.int32),
            pltpu.VMEM((2 * blocks, tok, BLK), F32),
            pltpu.VMEM((2 * blocks, tok, BLK), BF),
            pltpu.VMEM((2 * blocks, BLK, tok), BF),
            pltpu.SemaphoreType.DMA(()),
        ],
    )(me, own, r1, r2, oa, ob, *w, cotangent)
    other = swap(send, "c", "one")
    terms = lax.all_to_all(terms, "x", 0, 0)
    part = shape((ys // 2, META // 2, BLK), BF)
    g, hi_g, u, hi_u = call(first_kernel, (part,) * 4, [VMEM] * 2)(keep, other)
    from_g, from_u = swap(hi_g, "y", "two"), swap(hi_u, "y", "one")
    part = shape((ys // 4, META // 2, BLK), BF)
    g, hi_g, u, hi_u = call(second_kernel, (part,) * 4, [VMEM] * 4)(g, from_g, u, from_u)
    own = call(middle_kernel, shape(own.shape, BF), [VMEM, HBM])(terms, g)
    own = lax.all_to_all(own, "z", 0, 0)
    from_g, from_u = swap(hi_g, "y", "one"), swap(hi_u, "y", "two")
    part = shape((2, META // 2, BLK), BF)
    lo, hi = call(third_kernel, (part,) * 2, [VMEM] * 4)(g, from_g, u, from_u)
    other = swap(hi, "y", "far")
    grad_tokens = call(last_kernel, shape(tokens.shape, BF), [VMEM])(own)
    grad_gate, grad_up = call(
        unpack_kernel,
        (shape(gate_weight.shape, BF), shape(up_weight.shape, BF)),
        [SMEM, SMEM, VMEM, VMEM],
    )(gate_mask, up_mask, lo, other)
    return hidden, grad_tokens, grad_gate, grad_up


def solution(mesh):
    rows, cols = mesh.devices.shape
    cut = Mesh(mesh.devices.reshape(rows // 2, 2, 4, cols // 4), ("y", "c", "x", "z"))
    spec = P(("y", "c"), ("x", "z"))
    return jax.shard_map(
        body, mesh=cut, in_specs=(spec,) * 6, out_specs=(spec,) * 4, check_vma=False
    )
```

```python
import jax
import jax.numpy as jnp
from jax import lax
from jax.experimental import pallas as pl
from jax.experimental.pallas import tpu as pltpu
from jax.sharding import Mesh
from jax.sharding import PartitionSpec as P

BLK = 128
SLOTS = 4
META = SLOTS * BLK
BF = jnp.bfloat16
F32 = jnp.float32
VMEM = pl.BlockSpec(memory_space=pltpu.VMEM)
SMEM = pl.BlockSpec(memory_space=pltpu.SMEM)
HBM = pl.BlockSpec(memory_space=pltpu.HBM)


def call(kernel, outs, in_specs, scratch=(), out_spec=VMEM, limit=17):
    return pl.pallas_call(
        kernel,
        out_shape=outs,
        in_specs=in_specs,
        out_specs=jax.tree.map(lambda _: out_spec, outs),
        scratch_shapes=list(scratch),
        compiler_params=pltpu.CompilerParams(vmem_limit_bytes=limit * 1024 * 1024),
    )


def kept(mask_ref):
    cols = mask_ref.shape[1]
    first, second, count = jnp.int32(0), jnp.int32(0), jnp.int32(0)
    for p in range(mask_ref.shape[0] * cols):
        m = mask_ref[p // cols, p % cols]
        on = m == 1
        first = jnp.where(on & (count == 0), p, first)
        second = jnp.where(on & (count == 1), p, second)
        count = count + m
    return first, second, count


def block_of(ref, p, cols):
    r = pl.multiple_of((p // cols) * BLK, BLK)
    c = pl.multiple_of((p % cols) * BLK, BLK)
    return r, c


def turn(i, stage, size):
    if stage == "far":
        return (i + size // 2) % size
    if stage == "one":
        return i + 1 - 2 * (i % 2)
    return (i + size - 1 + 2 * (i % 2)) % size


def stages(size):
    return (["far"] if size > 4 else []) + ["one", "two"]


ORDERS = (["far", "one", "two"], ["far", "two", "one"])


def swap(x, axis, stage):
    size = lax.axis_size(axis)
    return lax.ppermute(x, axis, [(i, turn(i, stage, size)) for i in range(size)])


def origin(i, j, size, order=None):
    for bit, stage in reversed(list(enumerate(order or stages(size)))):
        if j >> bit & 1:
            i = turn(i, stage, size)
    return i


def pack_kernel(gm_ref, um_ref, tok_ref, gw_ref, uw_ref, out_ref, all_ref, gm, um, sems):
    cols = gm.shape[1]
    tokens = pltpu.make_async_copy(tok_ref, all_ref.at[0], sems.at[0])
    masks = [
        pltpu.make_async_copy(a, b, sems.at[1 + t])
        for t, (a, b) in enumerate(((gm_ref, gm), (um_ref, um)))
    ]
    for copy in masks + [tokens]:
        copy.start()
    for copy in masks:
        copy.wait()
    chosen = []
    for t, (m_ref, w_ref) in enumerate(((gm, gw_ref), (um, uw_ref))):
        first, second, count = kept(m_ref)
        for s, (p, on) in enumerate(((first, count >= 1), (second, count >= 2))):
            r, c = block_of(w_ref, p, cols)
            place = pl.ds((2 * t + s) * BLK, BLK)
            copy = pltpu.make_async_copy(
                w_ref.at[pl.ds(r, BLK), pl.ds(c, BLK)], out_ref.at[place], sems.at[3 + 2 * t + s]
            )
            copy.start()
            chosen.append((p, on, place, copy))
    lane = lax.broadcasted_iota(jnp.int32, (out_ref.shape[0] - META, BLK), 1)
    meta = jnp.zeros(lane.shape, jnp.int32)
    for s, (p, _, _, _) in enumerate(chosen):
        meta = jnp.where(lane == s, p, meta)
    out_ref[pl.ds(META, lane.shape[0]), :] = meta.astype(F32).astype(BF)
    tokens.wait()
    for z in range(1, all_ref.shape[0]):
        all_ref[z] = all_ref[0]
    for _, on, place, copy in chosen:
        copy.wait()

        @pl.when(jnp.logical_not(on))
        def _(place=place):
            out_ref[place, :] = jnp.zeros((BLK, BLK), BF)


def main_kernel(blocks, me_ref, own, r1, r2, oa, ob, w0, w1, w2, w3, cot_ref, *rest):
    hid_ref, keep_ref, send_ref, t_ref = rest[:4]
    x_ref, w_ref, metas, at_vec, at_ref, idx_ref, acc, g_ref, gt, sem, sems = rest[4:]
    my_x, my_c, my_y = me_ref[0], me_ref[1], me_ref[2]
    shards = w_ref.shape[0]
    ys, zs, half = shards // 2, own.shape[0], oa.shape[0]
    count = w0.shape[0]
    places, small, large = [], [], []
    for g, part in enumerate((w0, w1, w2, w3)):
        for i in range(count):
            k = g * count + i
            places.append(2 * origin(my_y, k % ys, ys) + (my_c if g < 2 else 1 - my_c))
            meta = part.at[i, pl.ds(META, 16)]
            small.append(pltpu.make_async_copy(meta, metas.at[k], sems.at[0, k]))
            data = part.at[i, pl.ds(0, META)]
            large.append(pltpu.make_async_copy(data, w_ref.at[places[k]], sems.at[1, k]))
    for copy in small + large:
        copy.start()
    xs = 2 * shards // zs
    far, one, two = ((turn(my_x, stage, xs)) for stage in ("far", "one", "two"))
    parts = ((own, my_x, 0), (r1, one, 0), (r2, two, 0), (oa, far, 0), (ob, far, half))
    for k, (part, x, z) in enumerate(parts):
        place = x_ref.at[pl.ds(x * zs + z, part.shape[0])]
        large.append(pltpu.make_async_copy(part, place, sems.at[2, k]))
        large[-1].start()
    for k, copy in enumerate(small):
        copy.wait()
        at_vec[pl.ds(k, 1), :] = metas[k].astype(F32).astype(jnp.int32)[:1]
    scalars = pltpu.make_async_copy(at_vec, at_ref, sem)
    scalars.start()
    scalars.wait()
    for k, n in enumerate(places):
        for s in range(SLOTS):
            idx_ref[n, s] = at_ref[k, s]
    for copy in large:
        copy.wait()

    acc[...] = jnp.zeros_like(acc)
    for n in range(shards):
        for s in range(SLOTS):
            p = idx_ref[n, s]
            a = p % blocks + (s // 2) * blocks
            acc[a] += jnp.dot(
                x_ref[2 * n + p // blocks],
                w_ref[n, pl.ds(s * BLK, BLK), :],
                preferred_element_type=F32,
            )
    for c in range(blocks):
        gate, up = acc[c], acc[blocks + c]
        lanes = pl.ds(c * BLK, BLK)
        cot = cot_ref[:, lanes].astype(F32)
        sigma = jax.nn.sigmoid(gate)
        hid_ref[:, lanes] = (gate * sigma * up).astype(BF)
        gg = cot * up * sigma * (1.0 + gate * (1.0 - sigma))
        gu = cot * gate * sigma
        g_ref[c] = gg.astype(BF)
        g_ref[blocks + c] = gu.astype(BF)
        gt[c] = gg.T.astype(BF)
        gt[blocks + c] = gu.T.astype(BF)
    for out_ref, core in ((send_ref, 1 - my_c), (keep_ref, my_c)):
        for t, order in enumerate(ORDERS):
            for j, s in ((j, s) for j in range(ys) for s in (2 * t, 2 * t + 1)):
                n = 2 * origin(my_y, j, ys, order) + core
                p = idx_ref[n, s]
                a = p % blocks + t * blocks
                out_ref[t, j, pl.ds((s - 2 * t) * BLK, BLK), :] = jnp.dot(
                    gt[a], x_ref[2 * n + p // blocks], preferred_element_type=F32
                ).astype(BF)
    for n in range(shards):
        sums = [None, None]
        for s in range(SLOTS):
            p = idx_ref[n, s]
            prod = lax.dot_general(
                g_ref[p % blocks + (s // 2) * blocks],
                w_ref[n, pl.ds(s * BLK, BLK), :],
                (((1,), (1,)), ((), ())),
                preferred_element_type=F32,
            )
            for r in range(2):
                add = jnp.where(p // blocks == r, prod, 0.0)
                sums[r] = add if sums[r] is None else sums[r] + add
        for r in range(2):
            k = 2 * n + r
            t_ref[k // zs, k % zs] = sums[r].astype(BF)


def total(parts):
    out = parts[0].astype(F32)
    for part in parts[1:]:
        out = out + part.astype(F32)
    return out


def halves(a_ref, b_ref, lo_ref, hi_ref):
    half = lo_ref.shape[0]
    for i in range(half):
        lo_ref[i] = total([a_ref[i], b_ref[i]]).astype(BF)
        hi_ref[i] = total([a_ref[half + i], b_ref[half + i]]).astype(BF)


def first_kernel(keep, other, lo_g, hi_g, lo_u, hi_u):
    halves(keep.at[0], other.at[0], lo_g, hi_g)
    halves(keep.at[1], other.at[1], lo_u, hi_u)


def second_kernel(g, from_g, u, from_u, lo_g, hi_g, lo_u, hi_u):
    halves(g, from_g, lo_g, hi_g)
    halves(u, from_u, lo_u, hi_u)


def third_kernel(g, from_g, u, from_u, lo, hi):
    halves(g, from_g, lo.at[pl.ds(0, 1)], hi.at[pl.ds(0, 1)])
    halves(u, from_u, lo.at[pl.ds(1, 1)], hi.at[pl.ds(1, 1)])


def middle_kernel(t_ref, _, out_ref):
    for z in range(out_ref.shape[0]):
        out_ref[z] = total([t_ref[x, z] for x in range(t_ref.shape[0])]).astype(BF)


def last_kernel(a_ref, out_ref):
    out_ref[...] = total([a_ref[z] for z in range(a_ref.shape[0])]).astype(BF)


def unpack_kernel(gm_ref, um_ref, a_ref, b_ref, gg_ref, gu_ref):
    cols = gm_ref.shape[1]
    for t, (m_ref, o_ref) in enumerate(((gm_ref, gg_ref), (um_ref, gu_ref))):
        o_ref[...] = jnp.zeros_like(o_ref)
        first, second, count = kept(m_ref)
        for s, (p, on) in enumerate(((first, count >= 1), (second, count >= 2))):

            @pl.when(on)
            def _(p=p, s=s):
                r, c = block_of(o_ref, p, cols)
                rows = pl.ds(s * BLK, BLK)
                block = total([a_ref[t, rows, :], b_ref[t, rows, :]])
                o_ref[pl.ds(r, BLK), pl.ds(c, BLK)] = block.T.astype(BF)


def body(tokens, gate_weight, up_weight, gate_mask, up_mask, cotangent):
    ys, xs, zs = (lax.axis_size(a) for a in ("y", "x", "z"))
    tok, width = cotangent.shape
    blocks = gate_mask.shape[1]
    half = zs // 2
    shape = jax.ShapeDtypeStruct
    me = jnp.stack([lax.axis_index(a) for a in ("x", "c", "y")]).astype(jnp.int32)

    packed, own = call(
        pack_kernel,
        (shape((META + 16, BLK), BF), shape((zs, tok, BLK), BF)),
        [HBM] * 5,
        [
            pltpu.SMEM(gate_mask.shape, jnp.int32),
            pltpu.SMEM(up_mask.shape, jnp.int32),
            pltpu.SemaphoreType.DMA((3 + SLOTS,)),
        ],
        limit=60,
    )(gate_mask, up_mask, tokens, gate_weight, up_weight)
    own = lax.all_to_all(own, "z", 0, 0)
    w = packed[None]
    *early, late = stages(ys)
    for stage in early:
        w = jnp.concatenate([w, swap(w, "y", stage)])
    w_late = swap(w, "y", late)
    r1, r2 = swap(own, "x", "one"), swap(own, "x", "two")
    w = [w, w_late, swap(w, "c", "one"), swap(w_late, "c", "one")]
    oa, ob = swap(r1[:half], "x", "two"), swap(r2[half:], "x", "one")

    hidden, keep, send, terms = call(
        lambda *refs: main_kernel(blocks, *refs),
        (
            shape((tok, width), BF),
            shape((2, ys, META // 2, BLK), BF),
            shape((2, ys, META // 2, BLK), BF),
            shape((xs, zs, tok, BLK), BF),
        ),
        [SMEM] + [HBM] * 9 + [VMEM],
        [
            pltpu.VMEM((xs * zs, tok, BLK), BF),
            pltpu.VMEM((2 * ys, META, BLK), BF),
            pltpu.VMEM((2 * ys, 16, BLK), BF),
            pltpu.VMEM((2 * ys, BLK), jnp.int32),
            pltpu.SMEM((2 * ys, BLK), jnp.int32),
            pltpu.SMEM((2 * ys, SLOTS), jnp.int32),
            pltpu.VMEM((2 * blocks, tok, BLK), F32),
            pltpu.VMEM((2 * blocks, tok, BLK), BF),
            pltpu.VMEM((2 * blocks, BLK, tok), BF),
            pltpu.SemaphoreType.DMA(()),
            pltpu.SemaphoreType.DMA((3, 2 * ys)),
        ],
        limit=58,
    )(me, own, r1, r2, oa, ob, *w, cotangent)
    other = swap(send, "c", "one")
    terms = lax.all_to_all(terms, "x", 0, 0)
    part = shape((ys // 2, META // 2, BLK), BF)
    g, hi_g, u, hi_u = call(first_kernel, (part,) * 4, [VMEM] * 2)(keep, other)
    from_g, from_u = swap(hi_g, "y", "two"), swap(hi_u, "y", "one")
    part = shape((ys // 4, META // 2, BLK), BF)
    g, hi_g, u, hi_u = call(second_kernel, (part,) * 4, [VMEM] * 4)(g, from_g, u, from_u)
    from_g, from_u = swap(hi_g, "y", "one"), swap(hi_u, "y", "two")
    part = shape((2, META // 2, BLK), BF)
    lo, hi = call(third_kernel, (part,) * 2, [VMEM] * 4)(g, from_g, u, from_u)
    own = call(middle_kernel, shape(own.shape, BF), [VMEM, HBM])(terms, lo)
    own = lax.all_to_all(own, "z", 0, 0)
    other = swap(hi, "y", "far")
    grad_tokens = call(last_kernel, shape(tokens.shape, BF), [VMEM])(own)
    grad_gate, grad_up = call(
        unpack_kernel,
        (shape(gate_weight.shape, BF), shape(up_weight.shape, BF)),
        [SMEM, SMEM, VMEM, VMEM],
    )(gate_mask, up_mask, lo, other)
    return hidden, grad_tokens, grad_gate, grad_up


def solution(mesh):
    rows, cols = mesh.devices.shape
    cut = Mesh(mesh.devices.reshape(rows // 2, 2, 4, cols // 4), ("y", "c", "x", "z"))
    spec = P(("y", "c"), ("x", "z"))
    return jax.shard_map(
        body, mesh=cut, in_specs=(spec,) * 6, out_specs=(spec,) * 4, check_vma=False
    )
```

```python
import jax
import jax.numpy as jnp
from jax import lax
from jax.experimental import pallas as pl
from jax.experimental.pallas import tpu as pltpu
from jax.sharding import Mesh
from jax.sharding import PartitionSpec as P

BLK = 128
SLOTS = 4
META = SLOTS * BLK
BF = jnp.bfloat16
F32 = jnp.float32
VMEM = pl.BlockSpec(memory_space=pltpu.VMEM)
SMEM = pl.BlockSpec(memory_space=pltpu.SMEM)
HBM = pl.BlockSpec(memory_space=pltpu.HBM)


def call(kernel, outs, in_specs, scratch=(), out_spec=VMEM, limit=17):
    return pl.pallas_call(
        kernel,
        out_shape=outs,
        in_specs=in_specs,
        out_specs=jax.tree.map(lambda _: out_spec, outs),
        scratch_shapes=list(scratch),
        compiler_params=pltpu.CompilerParams(vmem_limit_bytes=limit * 1024 * 1024),
    )


def kept(mask_ref):
    cols = mask_ref.shape[1]
    first, second, count = jnp.int32(0), jnp.int32(0), jnp.int32(0)
    for p in range(mask_ref.shape[0] * cols):
        m = mask_ref[p // cols, p % cols]
        on = m == 1
        first = jnp.where(on & (count == 0), p, first)
        second = jnp.where(on & (count == 1), p, second)
        count = count + m
    return first, second, count


def block_of(ref, p, cols):
    r = pl.multiple_of((p // cols) * BLK, BLK)
    c = pl.multiple_of((p % cols) * BLK, BLK)
    return r, c


def turn(i, stage, size):
    if stage == "far":
        return (i + size // 2) % size
    if stage == "one":
        return i + 1 - 2 * (i % 2)
    return (i + size - 1 + 2 * (i % 2)) % size


def stages(size):
    return (["far"] if size > 4 else []) + ["one", "two"]


ORDERS = (["far", "one", "two"], ["far", "two", "one"])


def swap(x, axis, stage):
    size = lax.axis_size(axis)
    return lax.ppermute(x, axis, [(i, turn(i, stage, size)) for i in range(size)])


def origin(i, j, size, order=None):
    for bit, stage in reversed(list(enumerate(order or stages(size)))):
        if j >> bit & 1:
            i = turn(i, stage, size)
    return i


def pack_kernel(gm_ref, um_ref, gw_ref, uw_ref, out_ref, gm, um, sems):
    cols = gm.shape[1]
    masks = [
        pltpu.make_async_copy(a, b, sems.at[t])
        for t, (a, b) in enumerate(((gm_ref, gm), (um_ref, um)))
    ]
    for copy in masks:
        copy.start()
    for copy in masks:
        copy.wait()
    chosen = []
    for t, (m_ref, w_ref) in enumerate(((gm, gw_ref), (um, uw_ref))):
        first, second, count = kept(m_ref)
        for s, (p, on) in enumerate(((first, count >= 1), (second, count >= 2))):
            r, c = block_of(w_ref, p, cols)
            place = pl.ds((2 * t + s) * BLK, BLK)
            copy = pltpu.make_async_copy(
                w_ref.at[pl.ds(r, BLK), pl.ds(c, BLK)], out_ref.at[place], sems.at[2 + 2 * t + s]
            )
            copy.start()
            chosen.append((p, on, place, copy))
    lane = lax.broadcasted_iota(jnp.int32, (out_ref.shape[0] - META, BLK), 1)
    meta = jnp.zeros(lane.shape, jnp.int32)
    for s, (p, _, _, _) in enumerate(chosen):
        meta = jnp.where(lane == s, p, meta)
    out_ref[pl.ds(META, lane.shape[0]), :] = meta.astype(F32).astype(BF)
    for _, on, place, copy in chosen:
        copy.wait()

        @pl.when(jnp.logical_not(on))
        def _(place=place):
            out_ref[place, :] = jnp.zeros((BLK, BLK), BF)


def main_kernel(blocks, me_ref, own, r1, r2, oa, ob, w0, w1, w2, w3, cot_ref, *rest):
    hid_ref, keep_ref, send_ref, t_ref = rest[:4]
    x_ref, w_ref, metas, at_vec, at_ref, idx_ref, acc, g_ref, gt, sem, sems = rest[4:]
    my_x, my_c, my_y, my_z = (me_ref[i] for i in range(4))
    shards = w_ref.shape[0]
    ys, zs, half = shards // 2, own.shape[0], oa.shape[0]
    count = w0.shape[0]
    places, small, large = [], [], []
    for g, part in enumerate((w0, w1, w2, w3)):
        for i in range(count):
            k = g * count + i
            places.append(2 * origin(my_y, k % ys, ys) + (my_c if g < 2 else 1 - my_c))
            meta = part.at[i, pl.ds(META, 16)]
            small.append(pltpu.make_async_copy(meta, metas.at[k], sems.at[0, k]))
            data = part.at[i, pl.ds(0, META)]
            large.append(pltpu.make_async_copy(data, w_ref.at[places[k]], sems.at[1, k]))
    for copy in small + large:
        copy.start()
    xs = 2 * shards // zs
    far, one, two = ((turn(my_x, stage, xs)) for stage in ("far", "one", "two"))
    parts = ((own, my_x, 0), (r1, one, 0), (r2, two, 0), (oa, far, 0), (ob, far, half))
    moves = [(part, i, x, z + i) for part, x, z in parts for i in range(part.shape[0])]
    for k, (part, i, x, j) in enumerate(moves):
        place = x_ref.at[x * zs + origin(my_z, j, zs)]
        sem_k = sems.at[2 + k // shards, k % shards]
        large.append(pltpu.make_async_copy(part.at[i], place, sem_k))
        large[-1].start()
    for k, copy in enumerate(small):
        copy.wait()
        at_vec[pl.ds(k, 1), :] = metas[k].astype(F32).astype(jnp.int32)[:1]
    scalars = pltpu.make_async_copy(at_vec, at_ref, sem)
    scalars.start()
    scalars.wait()
    for k, n in enumerate(places):
        for s in range(SLOTS):
            idx_ref[n, s] = at_ref[k, s]
    for copy in large:
        copy.wait()

    acc[...] = jnp.zeros_like(acc)
    for n in range(shards):
        for s in range(SLOTS):
            p = idx_ref[n, s]
            a = p % blocks + (s // 2) * blocks
            acc[a] += jnp.dot(
                x_ref[2 * n + p // blocks],
                w_ref[n, pl.ds(s * BLK, BLK), :],
                preferred_element_type=F32,
            )
    for c in range(blocks):
        gate, up = acc[c], acc[blocks + c]
        lanes = pl.ds(c * BLK, BLK)
        cot = cot_ref[:, lanes].astype(F32)
        sigma = jax.nn.sigmoid(gate)
        hid_ref[:, lanes] = (gate * sigma * up).astype(BF)
        gg = cot * up * sigma * (1.0 + gate * (1.0 - sigma))
        gu = cot * gate * sigma
        g_ref[c] = gg.astype(BF)
        g_ref[blocks + c] = gu.astype(BF)
        gt[c] = gg.T.astype(BF)
        gt[blocks + c] = gu.T.astype(BF)
    for out_ref, core in ((send_ref, 1 - my_c), (keep_ref, my_c)):
        for t, order in enumerate(ORDERS):
            for j, s in ((j, s) for j in range(ys) for s in (2 * t, 2 * t + 1)):
                n = 2 * origin(my_y, j, ys, order) + core
                p = idx_ref[n, s]
                a = p % blocks + t * blocks
                out_ref[t, j, pl.ds((s - 2 * t) * BLK, BLK), :] = jnp.dot(
                    gt[a], x_ref[2 * n + p // blocks], preferred_element_type=F32
                ).astype(BF)
    for n in range(shards):
        sums = [None, None]
        for s in range(SLOTS):
            p = idx_ref[n, s]
            prod = lax.dot_general(
                g_ref[p % blocks + (s // 2) * blocks],
                w_ref[n, pl.ds(s * BLK, BLK), :],
                (((1,), (1,)), ((), ())),
                preferred_element_type=F32,
            )
            for r in range(2):
                add = jnp.where(p // blocks == r, prod, 0.0)
                sums[r] = add if sums[r] is None else sums[r] + add
        for r in range(2):
            k = 2 * n + r
            t_ref[k // zs, k % zs] = sums[r].astype(BF)


def total(parts):
    out = parts[0].astype(F32)
    for part in parts[1:]:
        out = out + part.astype(F32)
    return out


def halves(a_ref, b_ref, lo_ref, hi_ref):
    half = lo_ref.shape[0]
    for i in range(half):
        lo_ref[i] = total([a_ref[i], b_ref[i]]).astype(BF)
        hi_ref[i] = total([a_ref[half + i], b_ref[half + i]]).astype(BF)


def first_kernel(keep, other, lo_g, hi_g, lo_u, hi_u):
    halves(keep.at[0], other.at[0], lo_g, hi_g)
    halves(keep.at[1], other.at[1], lo_u, hi_u)


def second_kernel(g, from_g, u, from_u, lo_g, hi_g, lo_u, hi_u):
    halves(g, from_g, lo_g, hi_g)
    halves(u, from_u, lo_u, hi_u)


def third_kernel(g, from_g, u, from_u, lo, hi):
    halves(g, from_g, lo.at[pl.ds(0, 1)], hi.at[pl.ds(0, 1)])
    halves(u, from_u, lo.at[pl.ds(1, 1)], hi.at[pl.ds(1, 1)])


def middle_kernel(t_ref, _, out_ref):
    for z in range(out_ref.shape[0]):
        out_ref[z] = total([t_ref[x, z] for x in range(t_ref.shape[0])]).astype(BF)


def last_kernel(a_ref, out_ref):
    out_ref[...] = total([a_ref[z] for z in range(a_ref.shape[0])]).astype(BF)


def unpack_kernel(gm_ref, um_ref, a_ref, b_ref, gg_ref, gu_ref):
    cols = gm_ref.shape[1]
    for t, (m_ref, o_ref) in enumerate(((gm_ref, gg_ref), (um_ref, gu_ref))):
        o_ref[...] = jnp.zeros_like(o_ref)
        first, second, count = kept(m_ref)
        for s, (p, on) in enumerate(((first, count >= 1), (second, count >= 2))):

            @pl.when(on)
            def _(p=p, s=s):
                r, c = block_of(o_ref, p, cols)
                rows = pl.ds(s * BLK, BLK)
                block = total([a_ref[t, rows, :], b_ref[t, rows, :]])
                o_ref[pl.ds(r, BLK), pl.ds(c, BLK)] = block.T.astype(BF)


def body(tokens, gate_weight, up_weight, gate_mask, up_mask, cotangent):
    ys, xs, zs = (lax.axis_size(a) for a in ("y", "x", "z"))
    tok, width = cotangent.shape
    blocks = gate_mask.shape[1]
    half = zs // 2
    shape = jax.ShapeDtypeStruct
    me = jnp.stack([lax.axis_index(a) for a in ("x", "c", "y", "z")]).astype(jnp.int32)

    packed = call(
        pack_kernel,
        shape((META + 16, BLK), BF),
        [HBM] * 4,
        [
            pltpu.SMEM(gate_mask.shape, jnp.int32),
            pltpu.SMEM(up_mask.shape, jnp.int32),
            pltpu.SemaphoreType.DMA((2 + SLOTS,)),
        ],
        limit=60,
    )(gate_mask, up_mask, gate_weight, up_weight)
    own = tokens[None]
    for stage in stages(zs):
        own = jnp.concatenate([own, swap(own, "z", stage)])
    w = packed[None]
    *early, late = stages(ys)
    for stage in early:
        w = jnp.concatenate([w, swap(w, "y", stage)])
    w_late = swap(w, "y", late)
    r1, r2 = swap(own, "x", "one"), swap(own, "x", "two")
    w = [w, w_late, swap(w, "c", "one"), swap(w_late, "c", "one")]
    oa, ob = swap(r1[:half], "x", "two"), swap(r2[half:], "x", "one")

    hidden, keep, send, terms = call(
        lambda *refs: main_kernel(blocks, *refs),
        (
            shape((tok, width), BF),
            shape((2, ys, META // 2, BLK), BF),
            shape((2, ys, META // 2, BLK), BF),
            shape((xs, zs, tok, BLK), BF),
        ),
        [SMEM] + [HBM] * 9 + [VMEM],
        [
            pltpu.VMEM((xs * zs, tok, BLK), BF),
            pltpu.VMEM((2 * ys, META, BLK), BF),
            pltpu.VMEM((2 * ys, 16, BLK), BF),
            pltpu.VMEM((2 * ys, BLK), jnp.int32),
            pltpu.SMEM((2 * ys, BLK), jnp.int32),
            pltpu.SMEM((2 * ys, SLOTS), jnp.int32),
            pltpu.VMEM((2 * blocks, tok, BLK), F32),
            pltpu.VMEM((2 * blocks, tok, BLK), BF),
            pltpu.VMEM((2 * blocks, BLK, tok), BF),
            pltpu.SemaphoreType.DMA(()),
            pltpu.SemaphoreType.DMA((4, 2 * ys)),
        ],
        limit=58,
    )(me, own, r1, r2, oa, ob, *w, cotangent)
    other = swap(send, "c", "one")
    terms = lax.all_to_all(terms, "x", 0, 0)
    part = shape((ys // 2, META // 2, BLK), BF)
    g, hi_g, u, hi_u = call(first_kernel, (part,) * 4, [VMEM] * 2)(keep, other)
    from_g, from_u = swap(hi_g, "y", "two"), swap(hi_u, "y", "one")
    part = shape((ys // 4, META // 2, BLK), BF)
    g, hi_g, u, hi_u = call(second_kernel, (part,) * 4, [VMEM] * 4)(g, from_g, u, from_u)
    from_g, from_u = swap(hi_g, "y", "one"), swap(hi_u, "y", "two")
    part = shape((2, META // 2, BLK), BF)
    lo, hi = call(third_kernel, (part,) * 2, [VMEM] * 4)(g, from_g, u, from_u)
    own = call(middle_kernel, shape(own.shape, BF), [VMEM, HBM])(terms, lo)
    own = lax.all_to_all(own, "z", 0, 0)
    other = swap(hi, "y", "far")
    grad_tokens = call(last_kernel, shape(tokens.shape, BF), [VMEM])(own)
    grad_gate, grad_up = call(
        unpack_kernel,
        (shape(gate_weight.shape, BF), shape(up_weight.shape, BF)),
        [SMEM, SMEM, VMEM, VMEM],
    )(gate_mask, up_mask, lo, other)
    return hidden, grad_tokens, grad_gate, grad_up


def solution(mesh):
    rows, cols = mesh.devices.shape
    cut = Mesh(mesh.devices.reshape(rows // 2, 2, 4, cols // 4), ("y", "c", "x", "z"))
    spec = P(("y", "c"), ("x", "z"))
    return jax.shard_map(
        body, mesh=cut, in_specs=(spec,) * 6, out_specs=(spec,) * 4, check_vma=False
    )
```

```python
import jax
import jax.numpy as jnp
from jax import lax
from jax.experimental import pallas as pl
from jax.experimental.pallas import tpu as pltpu
from jax.sharding import Mesh
from jax.sharding import PartitionSpec as P

BLK = 128
SLOTS = 4
META = SLOTS * BLK
BF = jnp.bfloat16
F32 = jnp.float32
VMEM = pl.BlockSpec(memory_space=pltpu.VMEM)
SMEM = pl.BlockSpec(memory_space=pltpu.SMEM)
HBM = pl.BlockSpec(memory_space=pltpu.HBM)


def call(kernel, outs, in_specs, scratch=(), out_spec=VMEM, limit=17):
    return pl.pallas_call(
        kernel,
        out_shape=outs,
        in_specs=in_specs,
        out_specs=jax.tree.map(lambda _: out_spec, outs),
        scratch_shapes=list(scratch),
        compiler_params=pltpu.CompilerParams(vmem_limit_bytes=limit * 1024 * 1024),
    )


def kept(mask_ref):
    cols = mask_ref.shape[1]
    first, second, count = jnp.int32(0), jnp.int32(0), jnp.int32(0)
    for p in range(mask_ref.shape[0] * cols):
        m = mask_ref[p // cols, p % cols]
        on = m == 1
        first = jnp.where(on & (count == 0), p, first)
        second = jnp.where(on & (count == 1), p, second)
        count = count + m
    return first, second, count


def block_of(ref, p, cols):
    r = pl.multiple_of((p // cols) * BLK, BLK)
    c = pl.multiple_of((p % cols) * BLK, BLK)
    return r, c


def turn(i, stage, size):
    if stage == "far":
        return (i + size // 2) % size
    if stage == "one":
        return i + 1 - 2 * (i % 2)
    return (i + size - 1 + 2 * (i % 2)) % size


def stages(size):
    return (["far"] if size > 4 else []) + ["one", "two"]


ORDERS = (["far", "one", "two"], ["far", "two", "one"])


def swap(x, axis, stage):
    size = lax.axis_size(axis)
    return lax.ppermute(x, axis, [(i, turn(i, stage, size)) for i in range(size)])


def origin(i, j, size, order=None):
    for bit, stage in reversed(list(enumerate(order or stages(size)))):
        if j >> bit & 1:
            i = turn(i, stage, size)
    return i


def pack_kernel(gm_ref, um_ref, tok_ref, gw_ref, uw_ref, out_ref, all_ref, gm, um, sems):
    cols = gm.shape[1]
    tokens = pltpu.make_async_copy(tok_ref, all_ref.at[0], sems.at[0])
    masks = [
        pltpu.make_async_copy(a, b, sems.at[1 + t])
        for t, (a, b) in enumerate(((gm_ref, gm), (um_ref, um)))
    ]
    for copy in masks + [tokens]:
        copy.start()
    for copy in masks:
        copy.wait()
    chosen = []
    for t, (m_ref, w_ref) in enumerate(((gm, gw_ref), (um, uw_ref))):
        first, second, count = kept(m_ref)
        for s, (p, on) in enumerate(((first, count >= 1), (second, count >= 2))):
            r, c = block_of(w_ref, p, cols)
            place = pl.ds((2 * t + s) * BLK, BLK)
            copy = pltpu.make_async_copy(
                w_ref.at[pl.ds(r, BLK), pl.ds(c, BLK)], out_ref.at[place], sems.at[3 + 2 * t + s]
            )
            copy.start()
            chosen.append((p, on, place, copy))
    lane = lax.broadcasted_iota(jnp.int32, (out_ref.shape[0] - META, BLK), 1)
    meta = jnp.zeros(lane.shape, jnp.int32)
    for s, (p, _, _, _) in enumerate(chosen):
        meta = jnp.where(lane == s, p, meta)
    out_ref[pl.ds(META, lane.shape[0]), :] = meta.astype(F32).astype(BF)
    tokens.wait()
    for z in range(1, all_ref.shape[0]):
        all_ref[z] = all_ref[0]
    for _, on, place, copy in chosen:
        copy.wait()

        @pl.when(jnp.logical_not(on))
        def _(place=place):
            out_ref[place, :] = jnp.zeros((BLK, BLK), BF)


def main_kernel(blocks, me_ref, own, r1, r2, oa, ob, w0, w1, w2, w3, cot_ref, *rest):
    hid_ref, keep_ref, send_ref, t_ref = rest[:4]
    x_ref, w_ref, metas, at_vec, at_ref, idx_ref, acc, g_ref, gt, sem, sems = rest[4:]
    my_x, my_c, my_y = me_ref[0], me_ref[1], me_ref[2]
    shards = w_ref.shape[0]
    ys, zs, half = shards // 2, own.shape[0], oa.shape[0]
    count = w0.shape[0]
    places, small, large = [], [], []
    for g, part in enumerate((w0, w1, w2, w3)):
        for i in range(count):
            k = g * count + i
            places.append(2 * origin(my_y, k % ys, ys) + (my_c if g < 2 else 1 - my_c))
            meta = part.at[i, pl.ds(META, 16)]
            small.append(pltpu.make_async_copy(meta, metas.at[k], sems.at[0, k]))
            data = part.at[i, pl.ds(0, META)]
            large.append(pltpu.make_async_copy(data, w_ref.at[places[k]], sems.at[1, k]))
    for copy in small + large:
        copy.start()
    xs = 2 * shards // zs
    far, one, two = ((turn(my_x, stage, xs)) for stage in ("far", "one", "two"))
    parts = ((own, my_x, 0), (r1, one, 0), (r2, two, 0), (oa, far, 0), (ob, far, half))
    for k, (part, x, z) in enumerate(parts):
        place = x_ref.at[pl.ds(x * zs + z, part.shape[0])]
        large.append(pltpu.make_async_copy(part, place, sems.at[2, k]))
        large[-1].start()
    for k, copy in enumerate(small):
        copy.wait()
        at_vec[pl.ds(k, 1), :] = metas[k].astype(F32).astype(jnp.int32)[:1]
    scalars = pltpu.make_async_copy(at_vec, at_ref, sem)
    scalars.start()
    scalars.wait()
    for k, n in enumerate(places):
        for s in range(SLOTS):
            idx_ref[n, s] = at_ref[k, s]
    acc[...] = jnp.zeros_like(acc)
    for copy in large[shards:]:
        copy.wait()
    for k, n in enumerate(places):
        large[k].wait()
        for s in range(SLOTS):
            p = at_ref[k, s]
            a = p % blocks + (s // 2) * blocks
            acc[a] += jnp.dot(
                x_ref[2 * n + p // blocks],
                w_ref[n, pl.ds(s * BLK, BLK), :],
                preferred_element_type=F32,
            )
    for c in range(blocks):
        gate, up = acc[c], acc[blocks + c]
        lanes = pl.ds(c * BLK, BLK)
        cot = cot_ref[:, lanes].astype(F32)
        sigma = jax.nn.sigmoid(gate)
        hid_ref[:, lanes] = (gate * sigma * up).astype(BF)
        gg = cot * up * sigma * (1.0 + gate * (1.0 - sigma))
        gu = cot * gate * sigma
        g_ref[c] = gg.astype(BF)
        g_ref[blocks + c] = gu.astype(BF)
        gt[c] = gg.T.astype(BF)
        gt[blocks + c] = gu.T.astype(BF)
    for out_ref, core in ((send_ref, 1 - my_c), (keep_ref, my_c)):
        for t, order in enumerate(ORDERS):
            for j, s in ((j, s) for j in range(ys) for s in (2 * t, 2 * t + 1)):
                n = 2 * origin(my_y, j, ys, order) + core
                p = idx_ref[n, s]
                a = p % blocks + t * blocks
                out_ref[t, j, pl.ds((s - 2 * t) * BLK, BLK), :] = jnp.dot(
                    gt[a], x_ref[2 * n + p // blocks], preferred_element_type=F32
                ).astype(BF)
    for n in range(shards):
        sums = [None, None]
        for s in range(SLOTS):
            p = idx_ref[n, s]
            prod = lax.dot_general(
                g_ref[p % blocks + (s // 2) * blocks],
                w_ref[n, pl.ds(s * BLK, BLK), :],
                (((1,), (1,)), ((), ())),
                preferred_element_type=F32,
            )
            for r in range(2):
                add = jnp.where(p // blocks == r, prod, 0.0)
                sums[r] = add if sums[r] is None else sums[r] + add
        for r in range(2):
            k = 2 * n + r
            t_ref[k // zs, k % zs] = sums[r].astype(BF)


def total(parts):
    out = parts[0].astype(F32)
    for part in parts[1:]:
        out = out + part.astype(F32)
    return out


def halves(a_ref, b_ref, lo_ref, hi_ref):
    half = lo_ref.shape[0]
    for i in range(half):
        lo_ref[i] = total([a_ref[i], b_ref[i]]).astype(BF)
        hi_ref[i] = total([a_ref[half + i], b_ref[half + i]]).astype(BF)


def first_kernel(keep, other, lo_g, hi_g, lo_u, hi_u):
    halves(keep.at[0], other.at[0], lo_g, hi_g)
    halves(keep.at[1], other.at[1], lo_u, hi_u)


def second_kernel(g, from_g, u, from_u, lo_g, hi_g, lo_u, hi_u):
    halves(g, from_g, lo_g, hi_g)
    halves(u, from_u, lo_u, hi_u)


def third_kernel(g, from_g, u, from_u, lo, hi):
    halves(g, from_g, lo.at[pl.ds(0, 1)], hi.at[pl.ds(0, 1)])
    halves(u, from_u, lo.at[pl.ds(1, 1)], hi.at[pl.ds(1, 1)])


def middle_kernel(t_ref, _, out_ref):
    for z in range(out_ref.shape[0]):
        out_ref[z] = total([t_ref[x, z] for x in range(t_ref.shape[0])]).astype(BF)


def last_kernel(a_ref, out_ref):
    out_ref[...] = total([a_ref[z] for z in range(a_ref.shape[0])]).astype(BF)


def unpack_kernel(gm_ref, um_ref, a_ref, b_ref, gg_ref, gu_ref):
    cols = gm_ref.shape[1]
    for t, (m_ref, o_ref) in enumerate(((gm_ref, gg_ref), (um_ref, gu_ref))):
        o_ref[...] = jnp.zeros_like(o_ref)
        first, second, count = kept(m_ref)
        for s, (p, on) in enumerate(((first, count >= 1), (second, count >= 2))):

            @pl.when(on)
            def _(p=p, s=s):
                r, c = block_of(o_ref, p, cols)
                rows = pl.ds(s * BLK, BLK)
                block = total([a_ref[t, rows, :], b_ref[t, rows, :]])
                o_ref[pl.ds(r, BLK), pl.ds(c, BLK)] = block.T.astype(BF)


def body(tokens, gate_weight, up_weight, gate_mask, up_mask, cotangent):
    ys, xs, zs = (lax.axis_size(a) for a in ("y", "x", "z"))
    tok, width = cotangent.shape
    blocks = gate_mask.shape[1]
    half = zs // 2
    shape = jax.ShapeDtypeStruct
    me = jnp.stack([lax.axis_index(a) for a in ("x", "c", "y")]).astype(jnp.int32)

    packed, own = call(
        pack_kernel,
        (shape((META + 16, BLK), BF), shape((zs, tok, BLK), BF)),
        [HBM] * 5,
        [
            pltpu.SMEM(gate_mask.shape, jnp.int32),
            pltpu.SMEM(up_mask.shape, jnp.int32),
            pltpu.SemaphoreType.DMA((3 + SLOTS,)),
        ],
        limit=60,
    )(gate_mask, up_mask, tokens, gate_weight, up_weight)
    own = lax.all_to_all(own, "z", 0, 0)
    w = packed[None]
    *early, late = stages(ys)
    for stage in early:
        w = jnp.concatenate([w, swap(w, "y", stage)])
    w_late = swap(w, "y", late)
    r1, r2 = swap(own, "x", "one"), swap(own, "x", "two")
    w = [w, w_late, swap(w, "c", "one"), swap(w_late, "c", "one")]
    oa, ob = swap(r1[:half], "x", "two"), swap(r2[half:], "x", "one")

    hidden, keep, send, terms = call(
        lambda *refs: main_kernel(blocks, *refs),
        (
            shape((tok, width), BF),
            shape((2, ys, META // 2, BLK), BF),
            shape((2, ys, META // 2, BLK), BF),
            shape((xs, zs, tok, BLK), BF),
        ),
        [SMEM] + [HBM] * 9 + [VMEM],
        [
            pltpu.VMEM((xs * zs, tok, BLK), BF),
            pltpu.VMEM((2 * ys, META, BLK), BF),
            pltpu.VMEM((2 * ys, 16, BLK), BF),
            pltpu.VMEM((2 * ys, BLK), jnp.int32),
            pltpu.SMEM((2 * ys, BLK), jnp.int32),
            pltpu.SMEM((2 * ys, SLOTS), jnp.int32),
            pltpu.VMEM((2 * blocks, tok, BLK), F32),
            pltpu.VMEM((2 * blocks, tok, BLK), BF),
            pltpu.VMEM((2 * blocks, BLK, tok), BF),
            pltpu.SemaphoreType.DMA(()),
            pltpu.SemaphoreType.DMA((3, 2 * ys)),
        ],
        limit=58,
    )(me, own, r1, r2, oa, ob, *w, cotangent)
    other = swap(send, "c", "one")
    terms = lax.all_to_all(terms, "x", 0, 0)
    part = shape((ys // 2, META // 2, BLK), BF)
    g, hi_g, u, hi_u = call(first_kernel, (part,) * 4, [VMEM] * 2)(keep, other)
    from_g, from_u = swap(hi_g, "y", "two"), swap(hi_u, "y", "one")
    part = shape((ys // 4, META // 2, BLK), BF)
    g, hi_g, u, hi_u = call(second_kernel, (part,) * 4, [VMEM] * 4)(g, from_g, u, from_u)
    from_g, from_u = swap(hi_g, "y", "one"), swap(hi_u, "y", "two")
    part = shape((2, META // 2, BLK), BF)
    lo, hi = call(third_kernel, (part,) * 2, [VMEM] * 4)(g, from_g, u, from_u)
    own = call(middle_kernel, shape(own.shape, BF), [VMEM, HBM])(terms, lo)
    own = lax.all_to_all(own, "z", 0, 0)
    other = swap(hi, "y", "far")
    grad_tokens = call(last_kernel, shape(tokens.shape, BF), [VMEM])(own)
    grad_gate, grad_up = call(
        unpack_kernel,
        (shape(gate_weight.shape, BF), shape(up_weight.shape, BF)),
        [SMEM, SMEM, VMEM, VMEM],
    )(gate_mask, up_mask, lo, other)
    return hidden, grad_tokens, grad_gate, grad_up


def solution(mesh):
    rows, cols = mesh.devices.shape
    cut = Mesh(mesh.devices.reshape(rows // 2, 2, 4, cols // 4), ("y", "c", "x", "z"))
    spec = P(("y", "c"), ("x", "z"))
    return jax.shard_map(
        body, mesh=cut, in_specs=(spec,) * 6, out_specs=(spec,) * 4, check_vma=False
    )
```
